32 devices in a mesh: layer: 4 (over y, core), phi: 8 (over z, x).
Axes of the slice: x: 2, y: 2, z: 4, core: 2. Of those that a mesh axis runs over, the one named last changes fastest.
Arguments:
- hit_features: bfloat16 [4, 8, 1024, 128], P('layer', 'phi'), may hold values from -6 to 6
- edge_features: bfloat16 [4, 8, 4, 1024, 128], P('layer', 'phi'), may hold values from -6 to 6
- sender_slot: int32 [4, 8, 4, 1024], P('layer', 'phi'), may hold values from 0 to 1023
- receiver_slot: int32 [4, 8, 4, 1024], P('layer', 'phi'), may hold values from 0 to 1023
- edge_count: int32 [4, 8, 4], P('layer', 'phi'), may hold values from 0 to 1024, as said below
- grad_hits: bfloat16 [4, 8, 1024, 128], P('layer', 'phi'), may hold values from -6 to 6
- grad_edges: bfloat16 [4, 8, 4, 1024, 128], P('layer', 'phi'), may hold values from -6 to 6
- w_edge_in: bfloat16 [384, 128], replicated, may hold values from -0.3125 to 0.3125
- w_edge_out: bfloat16 [128, 128], replicated, may hold values from -0.5 to 0.5
- w_node_in: bfloat16 [256, 128], replicated, may hold values from -0.375 to 0.375
- w_node_out: bfloat16 [128, 128], replicated, may hold values from -0.5 to 0.5
Outputs:
- hit_grads: float32 [4, 8, 1024, 128], P('layer', 'phi')
- edge_grads: bfloat16 [4, 8, 4, 1024, 128], P('layer', 'phi')
- edge_in_grad: float32 [384, 128], replicated
- edge_out_grad: float32 [128, 128], replicated
- node_in_grad: float32 [256, 128], replicated
- node_out_grad: float32 [128, 128], replicated
The draws below stay inside these ranges and needn't reach their ends.
Inputs may be any that keep to these rules, and one draw needn't show every extreme that they name: `edge_count`: live slots come first in each block. Kind 0 edges have their sender in the same shard, kind 1 in the previous layer group, kind 2 in the previous phi sector, kind 3 in the next one (phi closes into a loop). Kind 1 has no live slots in layer group 0. Some block is full in every draw. `sender_slot`: rows of dead slots are arbitrary. `receiver_slot`: rows of dead slots are arbitrary.
All inputs are finite; a program needn't handle non-finite values.
Results may differ from the reference program's by a relative error of at most 0.009.
Values may be sent and summed in bfloat16 or wider, within the bound.
No kernel may reach another device: no remote copies, remote signals or barrier semaphores. Data moves between devices by JAX's collectives and lax.ppermute only.
A program may use at most 64 MiB of HBM per device.

```python
import jax
import jax.numpy as jnp
from jax import lax

D = 128
KINDS = 4
NODE_DEV = 1024
EDGE_CAP = 1024
LAYERS = 4
SECTORS = 8
SHARDS = 32


def draw_edge_count(key, part):
    level_key, jitter_key, chosen_key = jax.random.split(key, 3)
    grid_shape = (LAYERS, SECTORS, KINDS)
    levels = jax.random.randint(level_key, grid_shape, 0, 3).astype(jnp.int32)
    full_rows = jnp.right_shift(jnp.full(grid_shape, EDGE_CAP, jnp.int32), levels)
    jitter = jax.random.randint(jitter_key, grid_shape, 0, 1 << 20).astype(jnp.int32) % (full_rows // 4 + 1)
    counts = full_rows - jitter
    chosen = jax.random.randint(chosen_key, (), 0, LAYERS * SECTORS).astype(jnp.int32)
    device_flat = jnp.arange(LAYERS * SECTORS, dtype=jnp.int32).reshape(LAYERS, SECTORS, 1)
    kind_index = jnp.arange(KINDS, dtype=jnp.int32).reshape(1, 1, KINDS)
    layer_index = jnp.arange(LAYERS, dtype=jnp.int32).reshape(LAYERS, 1, 1)
    counts = jnp.where((device_flat == chosen) & (kind_index == 0), EDGE_CAP, counts)
    counts = jnp.where((layer_index == 0) & (kind_index == 1), 0, counts)
    return counts.astype(jnp.int32)


def place_ends(result, key, low, top_value):
    longest = result.shape.index(max(result.shape))
    spots = []
    for shift in (0, 1):
        where = [jax.random.randint(jax.random.fold_in(key, axis), (), 0, length) for axis, length in enumerate(result.shape)]
        where[longest] = (where[longest] + shift) % result.shape[longest]
        spots.append(tuple(where))
    return result.at[spots[0]].set(low).at[spots[1]].set(top_value)


def shard_levels(rng, shape, shards, smallest, high):
    loudness = 1.0
    for position, parts in shards:
        draws = jax.random.uniform(jax.random.fold_in(jax.random.fold_in(rng, 6), position), (parts,), jnp.float32, smallest / len(shards), high / len(shards))
        loudness = loudness * jnp.repeat(jnp.exp(draws), shape[position] // parts).reshape((-1,) + (1,) * (len(shape) - 1 - position))
    return loudness


def gaussian(key, dims, scale, bound, cuts=(), kind=jnp.bfloat16):
    entries = scale * jax.random.normal(key, dims, jnp.float32)
    if cuts:
        entries = entries * shard_levels(key, dims, cuts, -0.22, 0.18)
    return jnp.clip(entries, -bound, bound).astype(kind)


def setup_inputs(seed: int = 0) -> dict:
    keys = jax.random.split(jax.random.key(seed), 12)
    hit_features = gaussian(keys[0], (LAYERS, SECTORS, NODE_DEV, D), 1.0, 6.0, ((0, 4), (1, 8)))
    edge_features = gaussian(keys[1], (LAYERS, SECTORS, KINDS, EDGE_CAP, D), 1.0, 6.0, ((0, 4), (1, 8)))
    sender_slot = place_ends(jax.random.randint(keys[2], (LAYERS, SECTORS, KINDS, EDGE_CAP), 0, NODE_DEV), jax.random.fold_in(keys[2], 1), 0, NODE_DEV - 1).astype(jnp.int32)
    receiver_slot = place_ends(jax.random.randint(keys[3], (LAYERS, SECTORS, KINDS, EDGE_CAP), 0, NODE_DEV), jax.random.fold_in(keys[3], 1), 0, NODE_DEV - 1).astype(jnp.int32)
    edge_count = draw_edge_count(jax.random.fold_in(keys[11], 71), 0)
    grad_hits = gaussian(keys[5], (LAYERS, SECTORS, NODE_DEV, D), 1.0, 6.0, ((0, 4), (1, 8)))
    grad_edges = gaussian(keys[6], (LAYERS, SECTORS, KINDS, EDGE_CAP, D), 1.0, 6.0, ((0, 4), (1, 8)))
    w_edge_in = gaussian(keys[7], (3 * D, D), (3 * D) ** -0.5, 0.3125)
    w_edge_out = gaussian(keys[8], (D, D), D ** -0.5, 0.5)
    w_node_in = gaussian(keys[9], (2 * D, D), (2 * D) ** -0.5, 0.375)
    w_node_out = gaussian(keys[10], (D, D), D ** -0.5, 0.5)
    return {"hit_features": hit_features, "edge_features": edge_features, "sender_slot": sender_slot, "receiver_slot": receiver_slot, "edge_count": edge_count, "grad_hits": grad_hits, "grad_edges": grad_edges, "w_edge_in": w_edge_in, "w_edge_out": w_edge_out, "w_node_in": w_node_in, "w_node_out": w_node_out}


norm_eps = 1e-05

def norm_act(pre_act):
    average = lax.optimization_barrier(jnp.mean(pre_act, axis=-1, keepdims=True))
    centred = pre_act - average
    spread = lax.optimization_barrier(jnp.mean(centred * centred, axis=-1, keepdims=True))
    scaled = centred * lax.rsqrt(spread + norm_eps)
    return scaled * jax.nn.sigmoid(scaled)

def norm_act_back(pre_act, upstream):
    _, pullback = jax.vjp(norm_act, pre_act)
    return pullback(upstream)[0]

def reference(hit_features, edge_features, sender_slot, receiver_slot, edge_count, grad_hits, grad_edges, w_edge_in, w_edge_out, w_node_in, w_node_out):
    positions = jnp.arange(EDGE_CAP, dtype=jnp.int32)

    def locate(device_flat):
        layer_at = device_flat // SECTORS
        sector_at = device_flat % SECTORS
        prev_sector = (sector_at + SECTORS - 1) % SECTORS
        next_sector = (sector_at + 1) % SECTORS
        lower_layer = jnp.maximum(layer_at - 1, 0)
        has_lower = layer_at > 0
        local_rows = hit_features[layer_at, sector_at]
        lower_rows = jnp.where(has_lower, hit_features[lower_layer, sector_at], jnp.zeros_like(local_rows))
        sources = (local_rows, lower_rows, hit_features[layer_at, prev_sector], hit_features[layer_at, next_sector])
        targets = ((layer_at, sector_at), (lower_layer, sector_at), (layer_at, prev_sector), (layer_at, next_sector))
        live_mask = (positions[None, :] < edge_count[layer_at, sector_at][:, None]).astype(jnp.float32)
        return (layer_at, sector_at, sources, targets, has_lower, live_mask)

    def forward_kind(sources, k, send_idx, recv_idx, edge_rows):
        inputs = jnp.concatenate([jnp.take(sources[k], send_idx, axis=0), jnp.take(sources[0], recv_idx, axis=0), edge_rows], axis=-1)
        pre_act = jnp.dot(inputs, w_edge_in, preferred_element_type=jnp.float32)
        hidden = norm_act(pre_act).astype(jnp.bfloat16)
        return (inputs, pre_act, hidden)

    def device_incoming(device_flat):
        layer_at, sector_at, sources, targets, has_lower, live_mask = locate(device_flat)
        incoming = jnp.zeros((NODE_DEV, D), jnp.float32)
        for k in range(KINDS):
            send_idx = sender_slot[layer_at, sector_at, k]
            recv_idx = receiver_slot[layer_at, sector_at, k]
            _, _, hidden = forward_kind(sources, k, send_idx, recv_idx, edge_features[layer_at, sector_at, k])
            message = jnp.dot(hidden, w_edge_out, preferred_element_type=jnp.float32) * live_mask[k][:, None]
            incoming = incoming + jax.ops.segment_sum(message, recv_idx, num_segments=NODE_DEV)
        return incoming.astype(jnp.bfloat16)
    devices_all = jnp.arange(SHARDS, dtype=jnp.int32)
    incoming = lax.map(device_incoming, devices_all).reshape(LAYERS, SECTORS, NODE_DEV, D)
    node_in = jnp.concatenate([hit_features, incoming], axis=-1).reshape(SHARDS * NODE_DEV, 2 * D)
    node_pre = jnp.dot(node_in, w_node_in, preferred_element_type=jnp.float32)
    node_hidden = norm_act(node_pre).astype(jnp.bfloat16)
    grad_flat = grad_hits.reshape(SHARDS * NODE_DEV, D)
    node_hidden_grad = jnp.dot(grad_flat, w_node_out.T, preferred_element_type=jnp.float32)
    node_out_grad = jnp.dot(node_hidden.T, grad_flat, preferred_element_type=jnp.float32) / SHARDS
    node_pre_grad = norm_act_back(node_pre, node_hidden_grad).astype(jnp.bfloat16)
    node_input_grad = jnp.dot(node_pre_grad, w_node_in.T, preferred_element_type=jnp.float32)
    node_in_grad = jnp.dot(node_in.T, node_pre_grad, preferred_element_type=jnp.float32) / SHARDS
    incoming_grad = node_input_grad[:, D:].reshape(LAYERS, SECTORS, NODE_DEV, D)
    hit_start = (grad_flat.astype(jnp.float32) + node_input_grad[:, :D]).reshape(LAYERS, SECTORS, NODE_DEV, D)

    def device_back(totals, device_flat):
        hit_total, in_total, out_total = totals
        layer_at, sector_at, sources, targets, has_lower, live_mask = locate(device_flat)
        recv_total = jnp.zeros((NODE_DEV, D), jnp.float32)
        edge_list = []
        for k in range(KINDS):
            send_idx = sender_slot[layer_at, sector_at, k]
            recv_idx = receiver_slot[layer_at, sector_at, k]
            grad_rows = grad_edges[layer_at, sector_at, k]
            inputs, pre_act, hidden = forward_kind(sources, k, send_idx, recv_idx, edge_features[layer_at, sector_at, k])
            message_grad = (live_mask[k][:, None] * (grad_rows.astype(jnp.float32) + jnp.take(incoming_grad[layer_at, sector_at], recv_idx, axis=0))).astype(jnp.bfloat16)
            hidden_grad = jnp.dot(message_grad, w_edge_out.T, preferred_element_type=jnp.float32)
            out_total = out_total + jnp.dot(hidden.T, message_grad, preferred_element_type=jnp.float32)
            pre_grad = norm_act_back(pre_act, hidden_grad).astype(jnp.bfloat16)
            input_grad = jnp.dot(pre_grad, w_edge_in.T, preferred_element_type=jnp.float32)
            in_total = in_total + jnp.dot(inputs.T, pre_grad, preferred_element_type=jnp.float32)
            edge_list.append((grad_rows.astype(jnp.float32) + input_grad[:, 2 * D:]).astype(jnp.bfloat16))
            recv_total = recv_total + jax.ops.segment_sum(input_grad[:, D:2 * D], recv_idx, num_segments=NODE_DEV)
            send_total = jax.ops.segment_sum(input_grad[:, :D], send_idx, num_segments=NODE_DEV)
            if k == 1:
                send_total = send_total * has_lower.astype(jnp.float32)
            target_layer, target_sector = targets[k]
            hit_total = hit_total.at[target_layer, target_sector].add(send_total)
        hit_total = hit_total.at[layer_at, sector_at].add(recv_total)
        return ((hit_total, in_total, out_total), jnp.stack(edge_list))
    start_totals = (hit_start, jnp.zeros((3 * D, D), jnp.float32), jnp.zeros((D, D), jnp.float32))
    (hit_grads, in_total, out_total), edge_grads = lax.scan(device_back, start_totals, devices_all)
    edge_grads = edge_grads.reshape(LAYERS, SECTORS, KINDS, EDGE_CAP, D)
    return (hit_grads, edge_grads, in_total / SHARDS, out_total / SHARDS, node_in_grad, node_out_grad)
```

```python
import functools

import jax
import jax.numpy as jnp
from jax import lax
from jax.experimental import pallas as pl
from jax.experimental.pallas import tpu as pltpu
from jax.sharding import PartitionSpec as P

norm_eps = 1e-05
bf16, f32 = jnp.bfloat16, jnp.float32
TILE = 256
VMEM_BYTES = 56 * 1024 * 1024


def shifted(value, axis, steps, ring):
    count = lax.axis_size(axis)
    if ring:
        route = [(i, (i + steps) % count) for i in range(count)]
    else:
        route = [(i, i + steps) for i in range(count) if 0 <= i + steps < count]
    return lax.ppermute(value, axis, route)


def dot(a, b):
    return jnp.dot(a, b, preferred_element_type=f32)


def dot_nt(a, b):
    return lax.dot_general(a, b, (((1,), (1,)), ((), ())), preferred_element_type=f32)


def dot_tn(a, b):
    return lax.dot_general(a, b, (((0,), (0,)), ((), ())), preferred_element_type=f32)


def halves(x):
    upper = x.astype(bf16)
    return upper, (x - upper.astype(f32)).astype(bf16)


def row_select(idx_row, nodes):
    edges = idx_row.shape[1]
    col = jnp.broadcast_to(idx_row, (128, edges)).T
    lane = lax.broadcasted_iota(jnp.int32, (edges, 128), 1)
    parts = [jnp.where(col == lane + c * 128, 1.0, 0.0).astype(bf16) for c in range(nodes // 128)]
    return jnp.concatenate(parts, axis=1)


def col_select(idx_row, nodes):
    edges = idx_row.shape[1]
    place = lax.broadcasted_iota(jnp.int32, (nodes, edges), 0)
    return jnp.where(place == idx_row, 1.0, 0.0).astype(bf16)


def normed(pre):
    centred = pre - jnp.mean(pre, axis=-1, keepdims=True)
    rstd = lax.rsqrt(jnp.mean(centred * centred, axis=-1, keepdims=True) + norm_eps)
    return centred * rstd, rstd


def gate(u):
    return 1.0 / (1.0 + jnp.exp(-u))


def normed_back(u, rstd, sig, upstream):
    du = upstream * (sig * (1.0 + u * (1.0 - sig)))
    mean_du = jnp.mean(du, axis=-1, keepdims=True)
    mean_duu = jnp.mean(du * u, axis=-1, keepdims=True)
    return rstd * (du - mean_du - u * mean_duu)


def live_rows(offset, count, shape):
    return offset + lax.broadcasted_iota(jnp.int32, shape, 0) < count


def idx_tile(ref, k, offset):
    return ref[k : k + 1, pl.ds(offset, TILE)]


def loop_tiles(count, step):
    def looped(i, carry):
        step(pl.multiple_of(i * TILE, TILE))
        return carry

    lax.fori_loop(0, (count + TILE - 1) // TILE, looped, 0)


def finish_forward(pre, offset, count, recv_row, nodes, u_ref, rs_ref, total_ref):
    u, rstd = normed(pre)
    u_ref[pl.ds(offset, TILE), :] = u
    rs_ref[pl.ds(offset, TILE), :] = jnp.broadcast_to(rstd, u.shape)
    hidden = jnp.where(live_rows(offset, count, u.shape), u * gate(u), 0.0).astype(bf16)
    total_ref[...] += dot(col_select(recv_row, nodes), hidden)


def first_kernel(counts, send, recv, hit, edges, w_in, part, u0, rs0, total):
    nodes, d = hit.shape
    kinds = send.shape[0]
    total[...] = jnp.zeros_like(total)
    for k in range(kinds):

        def step(offset, k=k):
            recv_row = idx_tile(recv, k, offset)
            rows = dot(row_select(recv_row, nodes), hit[...]).astype(bf16)
            pre = dot(rows, w_in[d : 2 * d, :]) + dot(
                edges[k, pl.ds(offset, TILE), :], w_in[2 * d :, :]
            )
            if k == 0:
                rows = dot(row_select(idx_tile(send, k, offset), nodes), hit[...]).astype(bf16)
                pre += dot(rows, w_in[:d, :])
                finish_forward(pre, offset, counts[k], recv_row, nodes, u0, rs0, total)
            else:
                part[k - 1, pl.ds(offset, TILE), :] = pre

        loop_tiles(counts[k], step)


def second_kernel(
    counts, send, recv, hit, src1, src2, src3, edges, grad_hit, grad_edge,
    w_in, w_out, wn_in, wn_out, part, u0, rs0, total0,
    back1, back2, back3, edge_done, hit_done, weights,
    u_s, rs_s, total, recv_sum, send_sum, inc_grad,
):
    nodes, d = hit.shape
    kinds = send.shape[0]
    sources = (hit, src1, src2, src3)
    us = (u0,) + tuple(u_s.at[k] for k in range(kinds - 1))
    rss = (rs0,) + tuple(rs_s.at[k] for k in range(kinds - 1))
    total[...] = total0[...]
    edge_done[...] = grad_edge[...]
    for k in range(1, kinds):

        def step(offset, k=k):
            rows = dot(row_select(idx_tile(send, k, offset), nodes), sources[k][...]).astype(bf16)
            pre = part[k - 1, pl.ds(offset, TILE), :] + dot(rows, w_in[:d, :])
            recv_row = idx_tile(recv, k, offset)
            finish_forward(pre, offset, counts[k], recv_row, nodes, us[k], rss[k], total)

        loop_tiles(counts[k], step)
    upper, lower = halves(total[...])
    incoming = (dot(upper, w_out[...]) + dot(lower, w_out[...])).astype(bf16)
    u, rstd = normed(dot(hit[...], wn_in[:d, :]) + dot(incoming, wn_in[d:, :]))
    sig = gate(u)
    hidden = (u * sig).astype(bf16)
    hidden_grad = dot_nt(grad_hit[...], wn_out[...])
    pre_grad = normed_back(u, rstd, sig, hidden_grad).astype(bf16)
    weights[6 * d : 7 * d, :] = dot_tn(hidden, grad_hit[...])
    weights[4 * d : 5 * d, :] = dot_tn(hit[...], pre_grad)
    weights[5 * d : 6 * d, :] = dot_tn(incoming, pre_grad)
    hit_done[...] = grad_hit[...].astype(f32) + dot_nt(pre_grad, wn_in[:d, :])
    upper, lower = halves(dot_nt(pre_grad, wn_in[d:, :]))
    inc_grad[:, :d] = upper
    inc_grad[:, d:] = lower
    recv_sum[...] = jnp.zeros_like(recv_sum)
    weights[: 4 * d, :] = jnp.zeros((4 * d, d), f32)
    for k in (*range(1, kinds), 0):
        send_sum[...] = jnp.zeros_like(send_sum)

        def step(offset, k=k):
            recv_row = idx_tile(recv, k, offset)
            picked = dot(row_select(recv_row, nodes), inc_grad[...])
            picked = picked[:, :d] + picked[:, d:]
            grad_rows = grad_edge[k, pl.ds(offset, TILE), :].astype(f32)
            live = live_rows(offset, counts[k], grad_rows.shape)
            message_grad = jnp.where(live, grad_rows + picked, 0.0).astype(bf16)
            hidden_grad = dot_nt(message_grad, w_out[...])
            u = us[k][pl.ds(offset, TILE), :]
            rstd = rss[k][pl.ds(offset, TILE), :]
            sig = gate(u)
            hidden = (u * sig).astype(bf16)
            pre_grad = normed_back(u, rstd, sig, hidden_grad).astype(bf16)
            edge_done[k, pl.ds(offset, TILE), :] = (
                grad_rows + dot_nt(pre_grad, w_in[2 * d :, :])
            ).astype(bf16)
            weights[2 * d : 3 * d, :] += dot_tn(edges[k, pl.ds(offset, TILE), :], pre_grad)
            weights[3 * d : 4 * d, :] += dot_tn(hidden, message_grad)
            recv_sum[...] += dot(col_select(recv_row, nodes), pre_grad)
            send_sum[...] += dot(col_select(idx_tile(send, k, offset), nodes), pre_grad)

        loop_tiles(counts[k], step)
        upper, lower = halves(send_sum[...])
        weights[:d, :] += dot_tn(sources[k][...], upper) + dot_tn(sources[k][...], lower)
        back = dot_nt(upper, w_in[:d, :]) + dot_nt(lower, w_in[:d, :])
        if k == 0:
            hit_done[...] += back
        else:
            (back1, back2, back3)[k - 1][...] = back.astype(bf16)
    upper, lower = halves(recv_sum[...])
    weights[d : 2 * d, :] = dot_tn(hit[...], upper) + dot_tn(hit[...], lower)
    hit_done[...] += dot_nt(upper, w_in[d : 2 * d, :]) + dot_nt(lower, w_in[d : 2 * d, :])


def on_device(kernel, outs, scratch, operands, flops):
    in_specs = [pl.BlockSpec(memory_space=pltpu.SMEM)]
    in_specs += [pl.BlockSpec(memory_space=pltpu.VMEM)] * (len(operands) - 1)
    return pl.pallas_call(
        kernel,
        out_shape=outs,
        in_specs=in_specs,
        out_specs=[pl.BlockSpec(memory_space=pltpu.VMEM)] * len(outs),
        scratch_shapes=scratch,
        compiler_params=pltpu.CompilerParams(vmem_limit_bytes=VMEM_BYTES),
        cost_estimate=pl.CostEstimate(flops=flops, bytes_accessed=4 << 20, transcendentals=1 << 20),
    )(*operands)


def all_summed(part, layers, sectors):
    axes = ("layer", "phi")
    total = layers * sectors
    if total & (total - 1) or layers < 2:
        return lax.psum(part, axes)

    def swap(value, mask):
        return lax.ppermute(value, axes, [(i, i ^ mask) for i in range(total)])

    rows, d = part.shape
    me = lax.axis_index("layer") % 2
    both = part.reshape(2, rows // 2, d)
    mine = lax.dynamic_index_in_dim(both, me, 0, False)
    other = lax.dynamic_index_in_dim(both, 1 - me, 0, False)
    mine = mine + swap(other.astype(bf16), sectors).astype(f32)
    bits = [1 << b for b in range(total.bit_length() - 1) if 1 << b != sectors]
    near = [1] + [b for b in bits if b > sectors]
    far = [b for b in bits if b not in near]
    ordered = far + near if len(far) % 2 == 0 else near + far
    for at in range(0, len(ordered), 2):
        pair = ordered[at : at + 2]
        masks = pair + [pair[0] ^ pair[1]] if len(pair) == 2 else pair
        sent = mine.astype(bf16)
        mine = sum((swap(sent, m).astype(f32) for m in masks), sent.astype(f32))
    mine = mine.astype(bf16)
    theirs = swap(mine, sectors)
    pair = jnp.where(me == 0, jnp.stack([mine, theirs]), jnp.stack([theirs, mine]))
    return pair.reshape(rows, d).astype(f32)


def body(
    hit_features, edge_features, sender_slot, receiver_slot, edge_count, grad_hits, grad_edges,
    w_edge_in, w_edge_out, w_node_in, w_node_out,
):
    hit = hit_features[0, 0]
    nodes, d = hit.shape
    edges, grad_edge = edge_features[0, 0], grad_edges[0, 0]
    send, recv, counts = sender_slot[0, 0], receiver_slot[0, 0], edge_count[0, 0]
    grad_hit = grad_hits[0, 0]
    kinds, cap = send.shape
    src1 = shifted(hit, "layer", 1, False)
    src2 = shifted(hit, "phi", 1, True)
    src3 = shifted(hit, "phi", -1, True)
    wide = jax.ShapeDtypeStruct((cap, d), f32)
    node_wide = jax.ShapeDtypeStruct((nodes, d), f32)
    part, u0, rs0, total0 = on_device(
        first_kernel,
        [jax.ShapeDtypeStruct((kinds - 1, cap, d), f32), wide, wide, node_wide],
        [],
        (counts, send, recv, hit, edges, w_edge_in),
        4 * 10**9,
    )
    back = jax.ShapeDtypeStruct((nodes, d), bf16)
    back1, back2, back3, edge_done, hit_done, weights = on_device(
        second_kernel,
        [
            back, back, back,
            jax.ShapeDtypeStruct(edges.shape, bf16),
            node_wide,
            jax.ShapeDtypeStruct((7 * d, d), f32),
        ],
        [
            pltpu.VMEM((kinds - 1, cap, d), f32),
            pltpu.VMEM((kinds - 1, cap, d), f32),
            pltpu.VMEM((nodes, d), f32),
            pltpu.VMEM((nodes, d), f32),
            pltpu.VMEM((nodes, d), f32),
            pltpu.VMEM((nodes, 2 * d), bf16),
        ],
        (counts, send, recv, hit, src1, src2, src3, edges, grad_hit, grad_edge,
         w_edge_in, w_edge_out, w_node_in, w_node_out, part, u0, rs0, total0),
        8 * 10**9,
    )
    layers, sectors = lax.axis_size("layer"), lax.axis_size("phi")
    from_upper = shifted(back1, "layer", -1, False).astype(f32)
    from_next = shifted(back2, "phi", -1, True).astype(f32)
    from_prev = shifted(back3, "phi", 1, True).astype(f32)
    summed = all_summed(weights, layers, sectors) / (layers * sectors)
    hit_total = hit_done + from_upper + (from_next + from_prev)
    return (
        hit_total[None, None],
        edge_done[None, None],
        summed[: 3 * d],
        summed[3 * d : 4 * d],
        summed[4 * d : 6 * d],
        summed[6 * d :],
    )


def solution(mesh):
    placed = (
        P("layer", "phi", None, None),
        P("layer", "phi", None, None, None),
        P("layer", "phi", None, None),
        P("layer", "phi", None, None),
        P("layer", "phi", None),
        P("layer", "phi", None, None),
        P("layer", "phi", None, None, None),
        P(),
        P(),
        P(),
        P(),
    )
    return jax.shard_map(
        body,
        mesh=mesh,
        in_specs=placed,
        out_specs=(
            P("layer", "phi", None, None),
            P("layer", "phi", None, None, None),
            P(),
            P(),
            P(),
            P(),
        ),
        check_vma=False,
    )
```

```python
import functools

import jax
import jax.numpy as jnp
from jax import lax
from jax.experimental import pallas as pl
from jax.experimental.pallas import tpu as pltpu
from jax.sharding import PartitionSpec as P

norm_eps = 1e-05
bf16, f32 = jnp.bfloat16, jnp.float32
SPAN = 256
VMEM_BYTES = 16 * 1024 * 1024


def shifted(value, axis, steps, ring):
    count = lax.axis_size(axis)
    if ring:
        route = [(i, (i + steps) % count) for i in range(count)]
    else:
        route = [(i, i + steps) for i in range(count) if 0 <= i + steps < count]
    return lax.ppermute(value, axis, route)


def dot(a, b):
    return jnp.dot(a, b, preferred_element_type=f32)


def dot_nt(a, b):
    return lax.dot_general(a, b, (((1,), (1,)), ((), ())), preferred_element_type=f32)


def dot_tn(a, b):
    return lax.dot_general(a, b, (((0,), (0,)), ((), ())), preferred_element_type=f32)


def halves(x):
    upper = x.astype(bf16)
    return upper, (x - upper.astype(f32)).astype(bf16)


def row_select(idx_row, nodes):
    edges = idx_row.shape[1]
    col = jnp.broadcast_to(idx_row, (128, edges)).T
    lane = lax.broadcasted_iota(jnp.int32, (edges, 128), 1)
    parts = [jnp.where(col == lane + c * 128, 1.0, 0.0).astype(bf16) for c in range(nodes // 128)]
    return jnp.concatenate(parts, axis=1)


def normed(pre):
    centred = pre - jnp.mean(pre, axis=-1, keepdims=True)
    rstd = lax.rsqrt(jnp.mean(centred * centred, axis=-1, keepdims=True) + norm_eps)
    return centred * rstd, rstd


def gate(u):
    return 1.0 / (1.0 + jnp.exp(-u))


def normed_back(u, rstd, sig, upstream):
    du = upstream * (sig * (1.0 + u * (1.0 - sig)))
    mean_du = jnp.mean(du, axis=-1, keepdims=True)
    mean_duu = jnp.mean(du * u, axis=-1, keepdims=True)
    return rstd * (du - mean_du - u * mean_duu)


class Tiles:
    def __init__(self, counts, kinds, cap, first, held):
        self.kinds, self.cap, self.first, self.held = kinds, cap, first, held
        self.counts = [counts[k] for k in kinds]
        self.ends = []
        end = jnp.int32(0)
        for count in self.counts:
            end = end + (count + SPAN - 1) // SPAN
            self.ends.append(end)

    def place(self, t):
        kind, at, start, count = self.kinds[0], jnp.int32(0), jnp.int32(0), self.counts[0]
        for i in range(1, len(self.kinds)):
            past = t >= self.ends[i - 1]
            kind = jnp.where(past, self.kinds[i], kind)
            at = jnp.where(past, i, at)
            start = jnp.where(past, self.ends[i - 1], start)
            count = jnp.where(past, self.counts[i], count)
        real = t < self.ends[-1]
        offset = jnp.where(real, (t - start) * SPAN, 0)
        rest = jnp.where(real, count - offset, 0)
        row = kind * self.cap + offset
        store = jnp.where(real, row - self.first * self.cap, self.held * self.cap)
        return Place(kind, at, offset, rest, row, store)

    def run(self, step):
        def looped(i, carry):
            step([self.place(2 * i), self.place(2 * i + 1)])
            return carry

        lax.fori_loop(0, (self.ends[-1] + 1) // 2, looped, 0)


class Place:
    def __init__(self, kind, at, offset, rest, row, store):
        self.kind, self.at, self.rest = kind, at, rest
        self.offset = pl.multiple_of(offset, SPAN)
        self.rows = pl.ds(pl.multiple_of(row, SPAN), SPAN)
        self.stored = pl.ds(pl.multiple_of(store, SPAN), SPAN)
        self.tile = store // SPAN

    def slots(self, ref):
        return ref[pl.ds(self.kind, 1), pl.ds(self.offset, SPAN)]


def rows_of(ref, places):
    return jnp.concatenate([ref[p.rows, :] for p in places], axis=0)


def slots_of(ref, places):
    return jnp.concatenate([p.slots(ref) for p in places], axis=1)


def live_of(places, d):
    place = lax.broadcasted_iota(jnp.int32, (SPAN, d), 0)
    return jnp.concatenate([place < p.rest for p in places], axis=0)


def store_rows(ref, places, value):
    for i, p in enumerate(places):
        ref[p.stored, :] = value[i * SPAN : (i + 1) * SPAN]


def receiver_forward(tiles, recv, hit, edges, w_in, part):
    nodes, d = hit.shape

    def step(places):
        picked = dot(row_select(slots_of(recv, places), nodes), hit[...]).astype(bf16)
        pre = dot(picked, w_in[d : 2 * d, :]) + dot(rows_of(edges, places), w_in[2 * d :, :])
        store_rows(part, places, pre)

    tiles.run(step)


def sender_part(places, send, source, w_in):
    nodes, d = source.shape[1:]
    picked = [dot(row_select(p.slots(send), nodes), source[p.at]) for p in places]
    return dot(jnp.concatenate(picked, axis=0).astype(bf16), w_in[:d, :])


def forward(tiles, send, recv, source, w_in, part, u_all, rs_all, hidden_all, total):
    d, nodes = total.shape

    def step(places):
        pre = rows_of(part, places)
        if source is not None:
            pre += sender_part(places, send, source, w_in)
        u, rstd = normed(pre)
        store_rows(u_all, places, u)
        store_rows(rs_all, places, jnp.broadcast_to(rstd, u.shape))
        hidden = jnp.where(live_of(places, d), u * gate(u), 0.0).T.astype(bf16)
        for i, p in enumerate(places):
            hidden_all[p.tile] = hidden[:, i * SPAN : (i + 1) * SPAN]
        total[...] += dot(hidden, row_select(slots_of(recv, places), nodes))

    tiles.run(step)


def local_kernel(
    counts_far, send_far, recv_far, hit_far, edges_far, w_in_far,
    part,
    counts, send, recv, hit, edges, w_in, arrived,
):
    far = (counts_far, send_far, recv_far, hit_far, edges_far, w_in_far)
    near = (counts, send, recv, hit.at[0], edges, w_in)
    copies = [pltpu.make_async_copy(f, n, arrived.at[i]) for i, (f, n) in enumerate(zip(far, near))]
    for copy in copies:
        copy.start()
    for copy in copies:
        copy.wait()
    kinds, cap = send.shape
    tiles = Tiles(counts, tuple(range(kinds)), cap, 0, kinds)
    receiver_forward(tiles, recv, hit.at[0], edges, w_in, part)

    def step(places):
        store_rows(part, places, rows_of(part, places) + sender_part(places, send, hit, w_in))

    Tiles(counts, (0,), cap, 0, kinds).run(step)


def early_kernel(
    counts, send, recv, src1, src2, w_in, part,
    u_all, rs_all, hidden_all, total,
    source,
):
    total[...] = jnp.zeros_like(total)
    source[0] = src1[...]
    source[1] = src2[...]
    cap = send.shape[1]
    results = (u_all, rs_all, hidden_all, total)
    forward(Tiles(counts, (0,), cap, 0, 3), send, recv, None, w_in, part, *results)
    forward(Tiles(counts, (1, 2), cap, 0, 3), send, recv, source, w_in, part, *results)


def both_halves(x, axis):
    return jnp.concatenate(halves(x), axis=axis)


def late_kernel(
    counts, send, recv, hit, src1, src2, src3, edges, grad_hit, grad_edge,
    w_in, w_out, wn_in, wn_out, part, u0, rs0, hidden0, total_in, me,
    back1, back2, back3, edge_back, recv_sum, send0, node_back, mine, other,
    source, send_sum, inc_grad, turned, weights, u_all, rs_all, hidden_all, total, moved,
):
    nodes, d = hit.shape
    kinds, cap = send.shape
    near, whole = cap // SPAN, 3 * cap // SPAN
    parts = (
        (u0.at[: 3 * cap], u_all.at[: 3 * cap]),
        (rs0.at[: 3 * cap], rs_all.at[: 3 * cap]),
        (hidden0.at[:whole], hidden_all.at[:whole]),
    )
    moves = [pltpu.make_async_copy(a, b, moved.at[i]) for i, (a, b) in enumerate(parts)]
    for move in moves:
        move.start()
    hidden_all[kinds * near] = jnp.zeros(hidden_all.shape[1:], bf16)
    total[...] = total_in[...]
    source[0] = src3[...]
    tiles = Tiles(counts, (3,), cap, 0, kinds)
    forward(tiles, send, recv, source, w_in, part, u_all, rs_all, hidden_all, total)
    for move in moves:
        move.wait()
    upper, lower = halves(total[...].T)
    incoming = (dot(upper, w_out[...]) + dot(lower, w_out[...])).astype(bf16)
    u, rstd = normed(dot(hit[...], wn_in[:d, :]) + dot(incoming, wn_in[d:, :]))
    sig = gate(u)
    hidden = (u * sig).astype(bf16)
    hidden_grad = dot_nt(grad_hit[...], wn_out[...])
    pre_grad = normed_back(u, rstd, sig, hidden_grad).astype(bf16)
    node_back[...] = pre_grad
    inc_grad[...] = both_halves(dot_nt(pre_grad, wn_in[d:, :]), 1)
    weights[6 * d : 7 * d, :] = dot_tn(hidden, grad_hit[...])
    weights[4 * d : 5 * d, :] = dot_tn(hit[...], pre_grad)
    weights[5 * d : 6 * d, :] = dot_tn(incoming, pre_grad)
    weights[3 * d : 4 * d, :] = jnp.zeros((d, d), f32)
    turned[...] = jnp.zeros_like(turned)
    recv_sum[...] = jnp.zeros_like(recv_sum)
    send_sum[...] = jnp.zeros_like(send_sum)

    def step(places):
        recv_hot = row_select(slots_of(recv, places), nodes)
        picked = dot(recv_hot, inc_grad[...])
        picked = picked[:, :d] + picked[:, d:]
        live = live_of(places, d)
        grad_rows = rows_of(grad_edge, places).astype(f32)
        message_grad = jnp.where(live, grad_rows + picked, 0.0).astype(bf16)
        hidden_grad = dot_nt(message_grad, w_out[...])
        u = rows_of(u_all, places)
        pre_grad = normed_back(u, rows_of(rs_all, places), gate(u), hidden_grad)
        pre_grad = jnp.where(live, pre_grad, 0.0)
        store_rows(edge_back, places, pre_grad.astype(bf16))
        pre_grad = pre_grad.T.astype(bf16)
        recv_sum[...] += dot(pre_grad, recv_hot)
        turned[...] += dot(pre_grad, rows_of(edges, places))
        hidden = jnp.concatenate([hidden_all[p.tile] for p in places], axis=1)
        weights[3 * d : 4 * d, :] += dot(hidden, message_grad)
        for i, p in enumerate(places):
            part_grad = pre_grad[:, i * SPAN : (i + 1) * SPAN]
            send_sum[p.kind] += dot(part_grad, row_select(p.slots(send), nodes))

    Tiles(counts, tuple(range(kinds)), cap, 0, kinds).run(step)
    weights[2 * d : 3 * d, :] = turned[...].T
    sources = (hit, src1, src2, src3)
    w_send = jnp.concatenate([w_in[:d, :], w_in[:d, :]], axis=1)
    send_turned = jnp.zeros((2 * d, d), f32)
    for k in range(kinds):
        both = both_halves(send_sum[k], 0)
        send_turned += dot(both, sources[k][...])
        if k > 0:
            (back1, back2, back3)[k - 1][...] = dot(w_send, both).T.astype(bf16)
    weights[:d, :] = (send_turned[:d] + send_turned[d:]).T
    recv_turned = dot(both_halves(recv_sum[...], 0), hit[...])
    weights[d : 2 * d, :] = (recv_turned[:d] + recv_turned[d:]).T
    send0[...] = send_sum[0]
    half = mine.shape[0]
    mine[...] = weights[pl.ds(pl.multiple_of(me[0] * half, half), half), :]
    other[...] = weights[pl.ds(pl.multiple_of((1 - me[0]) * half, half), half), :].astype(bf16)


def edge_kernel(
    counts, grad_hit, grad_edge, w_in, wn_in, edge_back, recv_sum, send0, node_back,
    edge_done, hit_done,
):
    d = w_in.shape[1]
    kinds, cap = edge_done.shape[:2]
    for k in range(kinds):
        rows = slice(k * cap, (k + 1) * cap)
        through = dot_nt(edge_back[rows, :], w_in[2 * d :, :])
        live = lax.broadcasted_iota(jnp.int32, through.shape, 0) < counts[k]
        edge_done[k] = (grad_edge[rows, :].astype(f32) + jnp.where(live, through, 0.0)).astype(bf16)
    ends = jnp.concatenate([w_in[d : 2 * d, :]] * 2 + [w_in[:d, :]] * 2, axis=1)
    sums = jnp.concatenate([both_halves(recv_sum[...], 0), both_halves(send0[...], 0)], axis=0)
    hit_done[...] = (
        grad_hit[...].astype(f32) + dot_nt(node_back[...], wn_in[:d, :]) + dot(ends, sums).T
    )


def closing_kernel(scale, me, mine, theirs, *outs):
    half = mine.shape[0]

    def put(block, start):
        row = 0
        for out in outs:
            low, high = max(row, start), min(row + out.shape[0], start + half)
            if low < high:
                out[low - row : high - row, :] = block[low - start : high - start, :].astype(f32) * scale
            row += out.shape[0]

    @pl.when(me[0] == 0)
    def _():
        put(mine, 0)
        put(theirs, half)

    @pl.when(me[0] != 0)
    def _():
        put(theirs, 0)
        put(mine, half)


def on_device(kernel, outs, operands, flops, scratch=(), scalars=(0,), hbm=False, free=()):
    vmem_spec = pl.BlockSpec(memory_space=pltpu.VMEM)
    smem_spec = pl.BlockSpec(memory_space=pltpu.SMEM)
    in_specs = [smem_spec if i in scalars else vmem_spec for i in range(len(operands))]
    if hbm:
        in_specs = [pl.BlockSpec(memory_space=pltpu.HBM)] * len(operands)
        operands = [pltpu.with_memory_space_constraint(x, pltpu.HBM) for x in operands]
    for i in free:
        in_specs[i] = pl.BlockSpec(memory_space=pl.ANY)
    return pl.pallas_call(
        kernel,
        out_shape=outs,
        in_specs=in_specs,
        out_specs=[vmem_spec] * len(outs),
        scratch_shapes=list(scratch),
        compiler_params=pltpu.CompilerParams(vmem_limit_bytes=VMEM_BYTES),
        cost_estimate=pl.CostEstimate(flops=flops, bytes_accessed=0, transcendentals=0),
    )(*operands)


def summed_over_chips(mine, total, sectors):
    axes = ("layer", "phi")

    def swap(value, mask):
        return lax.ppermute(value, axes, [(i, i ^ mask) for i in range(total)])

    bits = [1 << b for b in range(total.bit_length() - 1) if 1 << b != sectors]
    near = [1] + [b for b in bits if b > sectors]
    far = [b for b in bits if b not in near]
    ordered = far + near if len(far) % 2 == 0 else near + far
    for at in range(0, len(ordered), 2):
        pair = ordered[at : at + 2]
        masks = pair + [pair[0] ^ pair[1]] if len(pair) == 2 else pair
        sent = mine.astype(bf16)
        mine = sum((swap(sent, m).astype(f32) for m in masks), sent.astype(f32))
    mine = mine.astype(bf16)
    return mine, swap(mine, sectors)


def body(
    hit_features, edge_features, sender_slot, receiver_slot, edge_count, grad_hits, grad_edges,
    w_edge_in, w_edge_out, w_node_in, w_node_out,
):
    hit = hit_features[0, 0]
    nodes, d = hit.shape
    kinds, cap = sender_slot.shape[2:]
    edges, grad_edge = edge_features.reshape(kinds * cap, d), grad_edges.reshape(kinds * cap, d)
    send, recv, counts = sender_slot[0, 0], receiver_slot[0, 0], edge_count[0, 0]
    grad_hit = grad_hits[0, 0]
    layers, sectors = lax.axis_size("layer"), lax.axis_size("phi")
    devices = layers * sectors
    me = (lax.axis_index("layer") % 2).astype(jnp.int32).reshape(1)
    src2 = shifted(hit, "phi", 1, True)
    src3 = shifted(hit, "phi", -1, True)
    src1 = shifted(hit, "layer", 1, False)

    def shape(*dims, dtype=f32):
        return jax.ShapeDtypeStruct(dims, dtype)

    def rows(count):
        return shape(count * cap + SPAN, d)

    def tiles(count):
        return shape(count * cap // SPAN + 1, d, SPAN, dtype=bf16)

    turned = shape(d, nodes)
    node_half = shape(nodes, d, dtype=bf16)
    (part,) = on_device(
        local_kernel,
        [rows(kinds)],
        (counts, send, recv, hit, edges, w_edge_in),
        4 * 10**9,
        scratch=[
            pltpu.SMEM(counts.shape, jnp.int32),
            pltpu.VMEM(send.shape, jnp.int32),
            pltpu.VMEM(recv.shape, jnp.int32),
            pltpu.VMEM((1, nodes, d), bf16),
            pltpu.VMEM(edges.shape, bf16),
            pltpu.VMEM(w_edge_in.shape, bf16),
            pltpu.SemaphoreType.DMA((6,)),
        ],
        hbm=True,
    )
    u0, rs0, hidden0, total = on_device(
        early_kernel,
        [rows(3), rows(3), tiles(3), turned],
        (counts, send, recv, src1, src2, w_edge_in, part),
        2 * 10**9,
        scratch=[pltpu.VMEM((2, nodes, d), bf16)],
    )
    spare = kinds * cap + SPAN
    back1, back2, back3, edge_back, recv_sum, send0, node_back, mine, other = on_device(
        late_kernel,
        [
            node_half, node_half, node_half, shape(spare, d, dtype=bf16),
            turned, turned, node_half, shape(7 * d // 2, d), shape(7 * d // 2, d, dtype=bf16),
        ],
        (counts, send, recv, hit, src1, src2, src3, edges, grad_hit, grad_edge,
         w_edge_in, w_edge_out, w_node_in, w_node_out,
         part, u0, rs0, hidden0, total, me),
        8 * 10**9,
        scratch=[
            pltpu.VMEM((1, nodes, d), bf16),
            pltpu.VMEM((kinds, d, nodes), f32),
            pltpu.VMEM((nodes, 2 * d), bf16),
            pltpu.VMEM((d, d), f32),
            pltpu.VMEM((7 * d, d), f32),
            pltpu.VMEM((spare, d), f32),
            pltpu.VMEM((spare, d), f32),
            pltpu.VMEM((spare // SPAN, d, SPAN), bf16),
            pltpu.VMEM((d, nodes), f32),
            pltpu.SemaphoreType.DMA((3,)),
        ],
        scalars=(0, 19),
    )
    from_next = shifted(back2, "phi", -1, True)
    from_prev = shifted(back3, "phi", 1, True)
    from_upper = shifted(back1, "layer", -1, False)
    mine = mine + lax.ppermute(other, "layer", [(i, i ^ 1) for i in range(layers)]).astype(f32)
    edge_done, hit_done = on_device(
        edge_kernel,
        [shape(kinds, cap, d, dtype=bf16), shape(nodes, d)],
        (counts, grad_hit, grad_edge, w_edge_in, w_node_in,
         edge_back, recv_sum, send0, node_back),
        10**6,
    )
    mine, theirs = summed_over_chips(mine, devices, sectors)
    summed = on_device(
        functools.partial(closing_kernel, 1.0 / devices),
        [shape(3 * d, d), shape(d, d), shape(2 * d, d), shape(d, d)],
        (me, mine, theirs),
        10**6,
    )
    hit_total = hit_done + from_upper.astype(f32) + (from_next.astype(f32) + from_prev.astype(f32))
    return (hit_total[None, None], edge_done[None, None], *summed)


def solution(mesh):
    placed = (
        P("layer", "phi", None, None),
        P("layer", "phi", None, None, None),
        P("layer", "phi", None, None),
        P("layer", "phi", None, None),
        P("layer", "phi", None),
        P("layer", "phi", None, None),
        P("layer", "phi", None, None, None),
        P(),
        P(),
        P(),
        P(),
    )
    return jax.shard_map(
        body,
        mesh=mesh,
        in_specs=placed,
        out_specs=(
            P("layer", "phi", None, None),
            P("layer", "phi", None, None, None),
            P(),
            P(),
            P(),
            P(),
        ),
        check_vma=False,
    )
```

```python
import functools

import jax
import jax.numpy as jnp
from jax import lax
from jax.experimental import pallas as pl
from jax.experimental.pallas import tpu as pltpu
from jax.sharding import PartitionSpec as P

norm_eps = 1e-05
bf16, f32 = jnp.bfloat16, jnp.float32
SPAN = 256
VMEM_BYTES = 16 * 1024 * 1024


def shifted(value, axis, steps, ring):
    count = lax.axis_size(axis)
    if ring:
        route = [(i, (i + steps) % count) for i in range(count)]
    else:
        route = [(i, i + steps) for i in range(count) if 0 <= i + steps < count]
    return lax.ppermute(value, axis, route)


def dot(a, b):
    return jnp.dot(a, b, preferred_element_type=f32)


def dot_nt(a, b):
    return lax.dot_general(a, b, (((1,), (1,)), ((), ())), preferred_element_type=f32)


def dot_tn(a, b):
    return lax.dot_general(a, b, (((0,), (0,)), ((), ())), preferred_element_type=f32)


def halves(x):
    upper = x.astype(bf16)
    return upper, (x - upper.astype(f32)).astype(bf16)


def row_select(idx_row, nodes):
    edges = idx_row.shape[1]
    col = jnp.broadcast_to(idx_row, (128, edges)).T
    lane = lax.broadcasted_iota(jnp.int32, (edges, 128), 1)
    parts = [jnp.where(col == lane + c * 128, 1.0, 0.0).astype(bf16) for c in range(nodes // 128)]
    return jnp.concatenate(parts, axis=1)


def normed(pre):
    centred = pre - jnp.mean(pre, axis=-1, keepdims=True)
    rstd = lax.rsqrt(jnp.mean(centred * centred, axis=-1, keepdims=True) + norm_eps)
    return centred * rstd, rstd


def gate(u):
    return 1.0 / (1.0 + jnp.exp(-u))


def normed_back(u, rstd, sig, upstream):
    du = upstream * (sig * (1.0 + u * (1.0 - sig)))
    mean_du = jnp.mean(du, axis=-1, keepdims=True)
    mean_duu = jnp.mean(du * u, axis=-1, keepdims=True)
    return rstd * (du - mean_du - u * mean_duu)


class Tiles:
    def __init__(self, counts, kinds, cap, first, held):
        self.kinds, self.cap, self.first, self.held = kinds, cap, first, held
        self.counts = [counts[k] for k in kinds]
        self.ends = []
        end = jnp.int32(0)
        for count in self.counts:
            end = end + (count + SPAN - 1) // SPAN
            self.ends.append(end)

    def place(self, t):
        kind, at, start, count = self.kinds[0], jnp.int32(0), jnp.int32(0), self.counts[0]
        for i in range(1, len(self.kinds)):
            past = t >= self.ends[i - 1]
            kind = jnp.where(past, self.kinds[i], kind)
            at = jnp.where(past, i, at)
            start = jnp.where(past, self.ends[i - 1], start)
            count = jnp.where(past, self.counts[i], count)
        real = t < self.ends[-1]
        offset = jnp.where(real, (t - start) * SPAN, 0)
        rest = jnp.where(real, count - offset, 0)
        row = kind * self.cap + offset
        store = jnp.where(real, row - self.first * self.cap, self.held * self.cap)
        return Place(kind, at, offset, rest, row, row - self.first * self.cap, store)

    def run(self, step, group=2):
        def looped(i, carry):
            step([self.place(group * i + j) for j in range(group)])
            return carry

        lax.fori_loop(0, (self.ends[-1] + group - 1) // group, looped, 0)


class Place:
    def __init__(self, kind, at, offset, rest, row, own, store):
        self.kind, self.at, self.rest = kind, at, rest
        self.offset = pl.multiple_of(offset, SPAN)
        self.rows = pl.ds(pl.multiple_of(row, SPAN), SPAN)
        self.own = pl.ds(pl.multiple_of(own, SPAN), SPAN)
        self.stored = pl.ds(pl.multiple_of(store, SPAN), SPAN)
        self.tile = store // SPAN

    def slots(self, ref):
        return ref[pl.ds(self.kind, 1), pl.ds(self.offset, SPAN)]


def rows_of(ref, places):
    return jnp.concatenate([ref[p.rows, :] for p in places], axis=0)


def own_rows_of(ref, places):
    return jnp.concatenate([ref[p.own, :] for p in places], axis=0)


def slots_of(ref, places):
    return jnp.concatenate([p.slots(ref) for p in places], axis=1)


def live_of(places, d):
    place = lax.broadcasted_iota(jnp.int32, (SPAN, d), 0)
    return jnp.concatenate([place < p.rest for p in places], axis=0)


def store_rows(ref, places, value):
    for i, p in enumerate(places):
        ref[p.stored, :] = value[i * SPAN : (i + 1) * SPAN]


def receiver_forward(tiles, recv, hit, edges, w_in, part):
    nodes, d = hit.shape

    def step(places):
        picked = dot(row_select(slots_of(recv, places), nodes), hit[...]).astype(bf16)
        pre = dot(picked, w_in[d : 2 * d, :]) + dot(rows_of(edges, places), w_in[2 * d :, :])
        store_rows(part, places, pre)

    tiles.run(step, 4)


def sender_part(places, send, source, w_in):
    nodes, d = source.shape[1:]
    picked = [dot(row_select(p.slots(send), nodes), source[p.at]) for p in places]
    return dot(jnp.concatenate(picked, axis=0).astype(bf16), w_in[:d, :])


def forward(tiles, group, send, recv, source, w_in, part, u_all, rs_all, hidden_all, total):
    d, nodes = total.shape

    def step(places):
        pre = rows_of(part, places)
        if source is not None:
            pre += sender_part(places, send, source, w_in)
        u, rstd = normed(pre)
        store_rows(u_all, places, u)
        store_rows(rs_all, places, jnp.broadcast_to(rstd, u.shape))
        hidden = jnp.where(live_of(places, d), u * gate(u), 0.0).T.astype(bf16)
        for i, p in enumerate(places):
            hidden_all[p.tile] = hidden[:, i * SPAN : (i + 1) * SPAN]
        total[...] += dot(hidden, row_select(slots_of(recv, places), nodes))

    tiles.run(step, group)


def local_kernel(
    counts_far, send_far, recv_far, hit_far, edges_far, w_in_far,
    part,
    counts, send, recv, hit, edges, w_in, arrived,
):
    far = (counts_far, send_far, recv_far, hit_far, edges_far, w_in_far)
    near = (counts, send, recv, hit.at[0], edges, w_in)
    copies = [pltpu.make_async_copy(f, n, arrived.at[i]) for i, (f, n) in enumerate(zip(far, near))]
    for copy in copies:
        copy.start()
    for copy in copies:
        copy.wait()
    kinds, cap = send.shape
    tiles = Tiles(counts, tuple(range(kinds)), cap, 0, kinds)
    receiver_forward(tiles, recv, hit.at[0], edges, w_in, part)

    def step(places):
        store_rows(part, places, rows_of(part, places) + sender_part(places, send, hit, w_in))

    Tiles(counts, (0,), cap, 0, kinds).run(step, 4)


def early_kernel(
    counts, send, recv, src1, src2, w_in, part,
    u_all, rs_all, hidden_all, total,
    source,
):
    total[...] = jnp.zeros_like(total)
    hidden_all[hidden_all.shape[0] - 1] = jnp.zeros(hidden_all.shape[1:], bf16)
    source[0] = src1[...]
    source[1] = src2[...]
    cap = send.shape[1]
    results = (u_all, rs_all, hidden_all, total)
    forward(Tiles(counts, (0,), cap, 0, 3), 4, send, recv, None, w_in, part, *results)
    forward(Tiles(counts, (1, 2), cap, 0, 3), 4, send, recv, source, w_in, part, *results)


def both_halves(x, axis):
    return jnp.concatenate(halves(x), axis=axis)


def backward(
    tiles, send, recv, edges, grad_edge, w_out, inc_grad, u_all, rs_all, hidden_all,
    edge_back, recv_sum, send_sum, edge_turned, out_sum,
):
    nodes = inc_grad.shape[0]
    d = w_out.shape[0]

    def step(places):
        recv_hot = row_select(slots_of(recv, places), nodes)
        picked = dot(recv_hot, inc_grad[...])
        live = live_of(places, d)
        grad_rows = rows_of(grad_edge, places).astype(f32)
        message_grad = jnp.where(live, grad_rows + picked, 0.0).astype(bf16)
        hidden_grad = dot_nt(message_grad, w_out[...])
        u = own_rows_of(u_all, places)
        pre_grad = normed_back(u, own_rows_of(rs_all, places), gate(u), hidden_grad)
        pre_grad = jnp.where(live, pre_grad, 0.0)
        store_rows(edge_back, places, pre_grad.astype(bf16))
        pre_grad = pre_grad.T.astype(bf16)
        recv_sum[...] += dot(pre_grad, recv_hot)
        edge_turned[...] += dot(pre_grad, rows_of(edges, places))
        hidden = jnp.concatenate([hidden_all[p.tile] for p in places], axis=1)
        out_sum[...] += dot(hidden, message_grad)
        for i, p in enumerate(places):
            part_grad = pre_grad[:, i * SPAN : (i + 1) * SPAN]
            send_sum[p.at] += dot(part_grad, row_select(p.slots(send), nodes))

    tiles.run(step)


def senders_back(send_sum, w_in):
    d = w_in.shape[1]
    w_send = jnp.concatenate([w_in[:d, :], w_in[:d, :]], axis=1)
    return dot(w_send, both_halves(send_sum, 0)).T.astype(bf16)


def turned_product(sums, table):
    both = dot(both_halves(sums, 0), table)
    d = table.shape[1]
    return both[:d] + both[d:]


def node_kernel(
    counts, send, recv, hit, src2, src3, edges, grad_hit, grad_edge,
    w_in, w_out, wn_in, wn_out, part, u0, rs0, hidden0, total_in, me,
    far_back, near_back, edge_back, recv_sum, node_back, inc_grad, partial,
    source, send_sum, u_all, rs_all, hidden_all, total, moved,
):
    nodes, d = hit.shape
    cap = send.shape[1]
    near = cap // SPAN
    second = slice(2 * cap, 3 * cap)
    parts = (
        (u0.at[second], u_all.at[:cap]),
        (rs0.at[second], rs_all.at[:cap]),
        (hidden0.at[2 * near : 3 * near], hidden_all.at[:near]),
    )
    moves = [pltpu.make_async_copy(a, b, moved.at[i]) for i, (a, b) in enumerate(parts)]
    for move in moves:
        move.start()
    hidden_all[2 * near] = jnp.zeros(hidden_all.shape[1:], bf16)
    total[...] = total_in[...]
    source[0] = src3[...]
    results = (u_all, rs_all, hidden_all, total)
    forward(Tiles(counts, (3,), cap, 2, 2), 2, send, recv, source, w_in, part, *results)
    upper, lower = halves(total[...].T)
    incoming = (dot(upper, w_out[...]) + dot(lower, w_out[...])).astype(bf16)
    u, rstd = normed(dot(hit[...], wn_in[:d, :]) + dot(incoming, wn_in[d:, :]))
    sig = gate(u)
    hidden = (u * sig).astype(bf16)
    hidden_grad = dot_nt(grad_hit[...], wn_out[...])
    pre_grad = normed_back(u, rstd, sig, hidden_grad).astype(bf16)
    node_back[...] = pre_grad
    inc_grad[...] = dot_nt(pre_grad, wn_in[d:, :]).astype(bf16)
    partial[6 * d : 7 * d, :] = dot_tn(hidden, grad_hit[...])
    partial[4 * d : 5 * d, :] = dot_tn(hit[...], pre_grad)
    partial[5 * d : 6 * d, :] = dot_tn(incoming, pre_grad)
    partial[2 * d : 4 * d, :] = jnp.zeros((2 * d, d), f32)
    recv_sum[...] = jnp.zeros_like(recv_sum)
    send_sum[...] = jnp.zeros_like(send_sum)
    for move in moves:
        move.wait()
    backward(
        Tiles(counts, (2, 3), cap, 2, 2), send, recv, edges, grad_edge, w_out, inc_grad,
        u_all, rs_all, hidden_all, edge_back, recv_sum, send_sum,
        partial.at[2 * d : 3 * d], partial.at[3 * d : 4 * d],
    )
    partial[:d, :] = turned_product(send_sum[0], src2[...]) + turned_product(send_sum[1], src3[...])
    far_back[...] = senders_back(send_sum[me[1]], w_in)
    near_back[...] = senders_back(send_sum[1 - me[1]], w_in)


def last_kernel(
    counts, send, recv, hit, src1, edges, grad_edge, w_in, w_out,
    u0, rs0, hidden0, recv_in, inc_grad, partial, me,
    back1, edge_back, recv_sum, send0, mine, other,
    send_sum, weights,
):
    cap, d = send.shape[1], hit.shape[1]
    weights[...] = partial[...]
    recv_sum[...] = recv_in[...]
    send_sum[...] = jnp.zeros_like(send_sum)
    backward(
        Tiles(counts, (0, 1), cap, 0, 3), send, recv, edges, grad_edge, w_out, inc_grad,
        u0, rs0, hidden0, edge_back, recv_sum, send_sum,
        weights.at[2 * d : 3 * d], weights.at[3 * d : 4 * d],
    )
    turned = turned_product(send_sum[0], hit[...]) + turned_product(send_sum[1], src1[...])
    weights[:d, :] = (weights[:d, :] + turned).T
    weights[d : 2 * d, :] = turned_product(recv_sum[...], hit[...]).T
    weights[2 * d : 3 * d, :] = weights[2 * d : 3 * d, :].T
    back1[...] = senders_back(send_sum[1], w_in)
    send0[...] = send_sum[0]
    half = mine.shape[0]
    mine[...] = weights[pl.ds(pl.multiple_of(me[0] * half, half), half), :]
    other[...] = weights[pl.ds(pl.multiple_of((1 - me[0]) * half, half), half), :].astype(bf16)


def edge_kernel(
    counts, grad_hit, grad_edge, w_in, wn_in, first_back, second_back, recv_sum, send0, node_back,
    edge_done, hit_done,
):
    d = w_in.shape[1]
    kinds, cap = edge_done.shape[:2]
    for k in range(kinds):
        back = (first_back, second_back)[k // 2][k % 2 * cap : (k % 2 + 1) * cap, :]
        through = dot_nt(back, w_in[2 * d :, :])
        live = lax.broadcasted_iota(jnp.int32, through.shape, 0) < counts[k]
        grad_rows = grad_edge[k * cap : (k + 1) * cap, :].astype(f32)
        edge_done[k] = (grad_rows + jnp.where(live, through, 0.0)).astype(bf16)
    ends = jnp.concatenate([w_in[d : 2 * d, :]] * 2 + [w_in[:d, :]] * 2, axis=1)
    sums = jnp.concatenate([both_halves(recv_sum[...], 0), both_halves(send0[...], 0)], axis=0)
    hit_done[...] = (
        grad_hit[...].astype(f32) + dot_nt(node_back[...], wn_in[:d, :]) + dot(ends, sums).T
    )


def closing_kernel(scale, me, mine, theirs, *outs):
    half = mine.shape[0]

    def put(block, start):
        row = 0
        for out in outs:
            low, high = max(row, start), min(row + out.shape[0], start + half)
            if low < high:
                out[low - row : high - row, :] = block[low - start : high - start, :].astype(f32) * scale
            row += out.shape[0]

    @pl.when(me[0] == 0)
    def _():
        put(mine, 0)
        put(theirs, half)

    @pl.when(me[0] != 0)
    def _():
        put(theirs, 0)
        put(mine, half)


def on_device(kernel, outs, operands, flops, scratch=(), scalars=(0,), hbm=False, free=()):
    vmem_spec = pl.BlockSpec(memory_space=pltpu.VMEM)
    smem_spec = pl.BlockSpec(memory_space=pltpu.SMEM)
    in_specs = [smem_spec if i in scalars else vmem_spec for i in range(len(operands))]
    if hbm:
        in_specs = [pl.BlockSpec(memory_space=pltpu.HBM)] * len(operands)
        operands = [pltpu.with_memory_space_constraint(x, pltpu.HBM) for x in operands]
    for i in free:
        in_specs[i] = pl.BlockSpec(memory_space=pl.ANY)
    return pl.pallas_call(
        kernel,
        out_shape=outs,
        in_specs=in_specs,
        out_specs=[vmem_spec] * len(outs),
        scratch_shapes=list(scratch),
        compiler_params=pltpu.CompilerParams(vmem_limit_bytes=VMEM_BYTES),
        cost_estimate=pl.CostEstimate(flops=flops, bytes_accessed=0, transcendentals=0),
    )(*operands)


def summed_over_chips(mine, total, sectors, beside):
    axes = ("layer", "phi")

    def swap(value, mask):
        return lax.ppermute(value, axes, [(i, i ^ mask) for i in range(total)])

    bits = [1 << b for b in range(total.bit_length() - 1) if 1 << b != sectors]
    near = [1] + [b for b in bits if b > sectors]
    far = [b for b in bits if b not in near]
    ordered = far + near if len(far) % 2 == 0 else near + far
    for at in range(0, len(ordered), 2):
        pair = ordered[at : at + 2]
        masks = pair + [pair[0] ^ pair[1]] if len(pair) == 2 else pair
        sent = mine.astype(bf16)
        mine = sum((swap(sent, m).astype(f32) for m in masks), sent.astype(f32))
        if at == 0:
            mine, beside = lax.optimization_barrier((mine, beside))
    mine = mine.astype(bf16)
    return mine, swap(mine, sectors), beside


def body(
    hit_features, edge_features, sender_slot, receiver_slot, edge_count, grad_hits, grad_edges,
    w_edge_in, w_edge_out, w_node_in, w_node_out,
):
    hit = hit_features[0, 0]
    nodes, d = hit.shape
    kinds, cap = sender_slot.shape[2:]
    edges, grad_edge = edge_features.reshape(kinds * cap, d), grad_edges.reshape(kinds * cap, d)
    send, recv, counts = sender_slot[0, 0], receiver_slot[0, 0], edge_count[0, 0]
    grad_hit = grad_hits[0, 0]
    layers, sectors = lax.axis_size("layer"), lax.axis_size("phi")
    devices = layers * sectors
    me = jnp.stack([lax.axis_index("layer") % 2, lax.axis_index("phi") % 2]).astype(jnp.int32)
    src2 = shifted(hit, "phi", 1, True)
    src3 = shifted(hit, "phi", -1, True)
    src1 = shifted(hit, "layer", 1, False)

    def shape(*dims, dtype=f32):
        return jax.ShapeDtypeStruct(dims, dtype)

    def rows(count):
        return shape(count * cap + SPAN, d)

    def tiles(count):
        return shape(count * cap // SPAN + 1, d, SPAN, dtype=bf16)

    turned = shape(d, nodes)
    node_half = shape(nodes, d, dtype=bf16)
    (part,) = on_device(
        local_kernel,
        [rows(kinds)],
        (counts, send, recv, hit, edges, w_edge_in),
        4 * 10**9,
        scratch=[
            pltpu.SMEM(counts.shape, jnp.int32),
            pltpu.VMEM(send.shape, jnp.int32),
            pltpu.VMEM(recv.shape, jnp.int32),
            pltpu.VMEM((1, nodes, d), bf16),
            pltpu.VMEM(edges.shape, bf16),
            pltpu.VMEM(w_edge_in.shape, bf16),
            pltpu.SemaphoreType.DMA((6,)),
        ],
        hbm=True,
    )
    u0, rs0, hidden0, total = on_device(
        early_kernel,
        [rows(3), rows(3), tiles(3), turned],
        (counts, send, recv, src1, src2, w_edge_in, part),
        2 * 10**9,
        scratch=[pltpu.VMEM((2, nodes, d), bf16)],
    )
    partial = shape(7 * d, d)
    far_back, near_back, second_back, recv_sum, node_back, inc_grad, partial = on_device(
        node_kernel,
        [
            node_half, node_half, shape(2 * cap + SPAN, d, dtype=bf16),
            turned, node_half, node_half, partial,
        ],
        (counts, send, recv, hit, src2, src3, edges, grad_hit, grad_edge,
         w_edge_in, w_edge_out, w_node_in, w_node_out, part, u0, rs0, hidden0, total, me),
        8 * 10**9,
        scratch=[
            pltpu.VMEM((1, nodes, d), bf16),
            pltpu.VMEM((2, d, nodes), f32),
            pltpu.VMEM((2 * cap + SPAN, d), f32),
            pltpu.VMEM((2 * cap + SPAN, d), f32),
            pltpu.VMEM((2 * cap // SPAN + 1, d, SPAN), bf16),
            pltpu.VMEM((d, nodes), f32),
            pltpu.SemaphoreType.DMA((3,)),
        ],
        scalars=(0, 18),
    )
    route = [(i, (i + (2 if i % 2 else -2)) % sectors) for i in range(sectors)]
    relayed = lax.ppermute(far_back, "phi", route)
    back1, first_back, recv_sum, send0, mine, other = on_device(
        last_kernel,
        [
            node_half, shape(3 * cap + SPAN, d, dtype=bf16), turned, turned,
            shape(7 * d // 2, d), shape(7 * d // 2, d, dtype=bf16),
        ],
        (counts, send, recv, hit, src1, edges, grad_edge, w_edge_in, w_edge_out,
         u0, rs0, hidden0, recv_sum, inc_grad, partial, me),
        8 * 10**9,
        scratch=[pltpu.VMEM((2, d, nodes), f32), pltpu.VMEM((7 * d, d), f32)],
        scalars=(0, 15),
    )
    from_upper = shifted(back1, "layer", -1, False)
    other, relayed = lax.optimization_barrier((other, relayed))
    from_beside = lax.ppermute(
        (near_back.astype(f32) + relayed.astype(f32)).astype(bf16),
        "phi",
        [(i, i ^ 1) for i in range(sectors)],
    )
    mine = mine + lax.ppermute(other, "layer", [(i, i ^ 1) for i in range(layers)]).astype(f32)
    edge_done, hit_done = on_device(
        edge_kernel,
        [shape(kinds, cap, d, dtype=bf16), shape(nodes, d)],
        (counts, grad_hit, grad_edge, w_edge_in, w_node_in,
         first_back, second_back, recv_sum, send0, node_back),
        10**6,
    )
    hit_total = hit_done + from_upper.astype(f32) + from_beside.astype(f32)
    mine, theirs, hit_total = summed_over_chips(mine, devices, sectors, hit_total)
    summed = on_device(
        functools.partial(closing_kernel, 1.0 / devices),
        [shape(3 * d, d), shape(d, d), shape(2 * d, d), shape(d, d)],
        (me, mine, theirs),
        10**6,
    )
    return (hit_total[None, None], edge_done[None, None], *summed)


def solution(mesh):
    placed = (
        P("layer", "phi", None, None),
        P("layer", "phi", None, None, None),
        P("layer", "phi", None, None),
        P("layer", "phi", None, None),
        P("layer", "phi", None),
        P("layer", "phi", None, None),
        P("layer", "phi", None, None, None),
        P(),
        P(),
        P(),
        P(),
    )
    return jax.shard_map(
        body,
        mesh=mesh,
        in_specs=placed,
        out_specs=(
            P("layer", "phi", None, None),
            P("layer", "phi", None, None, None),
            P(),
            P(),
            P(),
            P(),
        ),
        check_vma=False,
    )
```

```python
import functools

import jax
import jax.numpy as jnp
from jax import lax
from jax.experimental import pallas as pl
from jax.experimental.pallas import tpu as pltpu
from jax.sharding import PartitionSpec as P

norm_eps = 1e-05
bf16, f32 = jnp.bfloat16, jnp.float32
SPAN = 256
FOLD = 4
FORWARD = 2
BACKWARD = 2
VMEM_BYTES = 16 * 1024 * 1024


def shifted(value, axis, steps, ring):
    count = lax.axis_size(axis)
    if ring:
        route = [(i, (i + steps) % count) for i in range(count)]
    else:
        route = [(i, i + steps) for i in range(count) if 0 <= i + steps < count]
    return lax.ppermute(value, axis, route)


def dot(a, b):
    return jnp.dot(a, b, preferred_element_type=f32)


def dot_nt(a, b):
    return lax.dot_general(a, b, (((1,), (1,)), ((), ())), preferred_element_type=f32)


def dot_tn(a, b):
    return lax.dot_general(a, b, (((0,), (0,)), ((), ())), preferred_element_type=f32)


def halves(x):
    upper = x.astype(bf16)
    return upper, (x - upper.astype(f32)).astype(bf16)


def folded(table):
    width = table.shape[0] // FOLD
    return jnp.concatenate([table[f * width : (f + 1) * width] for f in range(FOLD)], axis=1)


def unfolded_sums(sums):
    d = sums.shape[0] // FOLD
    return jnp.concatenate([sums[f * d : (f + 1) * d] for f in range(FOLD)], axis=1)


class Slots:
    def __init__(self, idx_row, nodes):
        edges = idx_row.shape[1]
        chunks = nodes // FOLD // 128
        block = idx_row >> 7
        self.part = block // chunks
        low = jnp.broadcast_to((idx_row & 127).astype(f32).astype(bf16), (128, edges)).T
        chunk = (block - self.part * chunks).astype(f32).astype(bf16)
        chunk = jnp.broadcast_to(chunk, (128, edges)).T
        self.part_rows = jnp.broadcast_to(self.part.astype(f32), (128, edges)).T
        lane = lax.broadcasted_iota(jnp.int32, (edges, 128), 1).astype(f32).astype(bf16)
        one = jnp.where(low == lane, bf16(1), bf16(0))
        hots = [jnp.where(chunk == bf16(c), one, bf16(0)) for c in range(chunks)]
        self.hot = jnp.concatenate(hots, axis=1)

    def rows(self, table):
        wide = dot(self.hot, table)
        d = wide.shape[1] // FOLD
        out = wide[:, :d]
        for f in range(1, FOLD):
            out = jnp.where(self.part_rows == f, wide[:, f * d : (f + 1) * d], out)
        return out

    def sums(self, turned):
        parts = [jnp.where(self.part == f, turned, 0.0).astype(bf16) for f in range(FOLD)]
        return dot(jnp.concatenate(parts, axis=0), self.hot)


def normed(pre):
    centred = pre - jnp.mean(pre, axis=-1, keepdims=True)
    rstd = lax.rsqrt(jnp.mean(centred * centred, axis=-1, keepdims=True) + norm_eps)
    return centred * rstd, rstd


def gate(u):
    return 1.0 / (1.0 + jnp.exp(-u))


def normed_back(u, rstd, sig, upstream):
    du = upstream * (sig * (1.0 + u * (1.0 - sig)))
    mean_du = jnp.mean(du, axis=-1, keepdims=True)
    mean_duu = jnp.mean(du * u, axis=-1, keepdims=True)
    return rstd * (du - mean_du - u * mean_duu)


class Tiles:
    def __init__(self, counts, kinds, cap, first, held):
        self.kinds, self.cap, self.first, self.held = kinds, cap, first, held
        self.counts = [counts[k] for k in kinds]
        self.ends = []
        end = jnp.int32(0)
        for count in self.counts:
            end = end + (count + SPAN - 1) // SPAN
            self.ends.append(end)

    def place(self, t):
        kind, at, start, count = self.kinds[0], jnp.int32(0), jnp.int32(0), self.counts[0]
        for i in range(1, len(self.kinds)):
            past = t >= self.ends[i - 1]
            kind = jnp.where(past, self.kinds[i], kind)
            at = jnp.where(past, i, at)
            start = jnp.where(past, self.ends[i - 1], start)
            count = jnp.where(past, self.counts[i], count)
        real = t < self.ends[-1]
        offset = jnp.where(real, (t - start) * SPAN, 0)
        rest = jnp.where(real, count - offset, 0)
        row = kind * self.cap + offset
        store = jnp.where(real, row - self.first * self.cap, self.held * self.cap)
        return Place(kind, at, offset, rest, row, row - self.first * self.cap, store)

    def pipelined(self, front, back, held, group):
        steps = (self.ends[-1] + group - 1) // group

        def places(i):
            return [self.place(group * i + j) for j in range(group)]

        def looped(i, carry):
            back(places(i - 1), held[...])
            held[...] = front(places(i))
            return carry

        @pl.when(steps > 0)
        def _():
            held[...] = front(places(0))
            lax.fori_loop(1, steps, looped, 0)
            back(places(steps - 1), held[...])

    def run(self, step, group=2):
        def looped(i, carry):
            step([self.place(group * i + j) for j in range(group)])
            return carry

        lax.fori_loop(0, (self.ends[-1] + group - 1) // group, looped, 0)


class Place:
    def __init__(self, kind, at, offset, rest, row, own, store):
        self.kind, self.at, self.rest = kind, at, rest
        self.offset = pl.multiple_of(offset, SPAN)
        self.rows = pl.ds(pl.multiple_of(row, SPAN), SPAN)
        self.own = pl.ds(pl.multiple_of(own, SPAN), SPAN)
        self.stored = pl.ds(pl.multiple_of(store, SPAN), SPAN)
        self.tile = store // SPAN

    def slots(self, ref):
        return ref[pl.ds(self.kind, 1), pl.ds(self.offset, SPAN)]


def rows_of(ref, places):
    return jnp.concatenate([ref[p.rows, :] for p in places], axis=0)


def own_rows_of(ref, places):
    return jnp.concatenate([ref[p.own, :] for p in places], axis=0)


def slots_of(ref, places):
    return jnp.concatenate([p.slots(ref) for p in places], axis=1)


def live_of(places, d):
    place = lax.broadcasted_iota(jnp.int32, (SPAN, d), 0)
    return jnp.concatenate([place < p.rest for p in places], axis=0)


def store_rows(ref, places, value):
    for i, p in enumerate(places):
        ref[p.stored, :] = value[i * SPAN : (i + 1) * SPAN]


def receiver_forward(tiles, recv, table, edges, w_in, part):
    nodes, d = table.shape[0] * FOLD, w_in.shape[1]

    def step(places):
        picked = Slots(slots_of(recv, places), nodes).rows(table[...]).astype(bf16)
        pre = dot(picked, w_in[d : 2 * d, :]) + dot(rows_of(edges, places), w_in[2 * d :, :])
        store_rows(part, places, pre)

    tiles.run(step, 4)


def sender_part(places, send, source, w_in):
    nodes, d = source.shape[1] * FOLD, w_in.shape[1]
    picked = [Slots(p.slots(send), nodes).rows(source[p.at]) for p in places]
    return dot(jnp.concatenate(picked, axis=0).astype(bf16), w_in[:d, :])


def forward(tiles, send, recv, source, w_in, part, held, u_all, rs_all, hidden_all, total):
    d = w_in.shape[1]
    nodes = total.shape[1] * FOLD

    def front(places):
        pre = rows_of(part, places)
        if source is not None:
            pre += sender_part(places, send, source, w_in)
        u, rstd = normed(pre)
        store_rows(u_all, places, u)
        store_rows(rs_all, places, jnp.broadcast_to(rstd, u.shape))
        hidden = jnp.where(live_of(places, d), u * gate(u), 0.0).T
        for i, p in enumerate(places):
            hidden_all[p.tile] = hidden[:, i * SPAN : (i + 1) * SPAN].astype(bf16)
        return hidden

    def back(places, hidden):
        total[...] += Slots(slots_of(recv, places), nodes).sums(hidden)

    tiles.pipelined(front, back, held, FORWARD)


def local_kernel(
    counts_far, send_far, recv_far, hit_far, edges_far, w_in_far,
    part,
    counts, send, recv, hit, edges, w_in, table, arrived,
):
    far = (counts_far, send_far, recv_far, hit_far, edges_far, w_in_far)
    near = (counts, send, recv, hit, edges, w_in)
    copies = [pltpu.make_async_copy(f, n, arrived.at[i]) for i, (f, n) in enumerate(zip(far, near))]
    for copy in copies:
        copy.start()
    for copy in copies:
        copy.wait()
    table[0] = folded(hit[...])
    kinds, cap = send.shape
    tiles = Tiles(counts, tuple(range(kinds)), cap, 0, kinds)
    receiver_forward(tiles, recv, table.at[0], edges, w_in, part)

    def step(places):
        store_rows(part, places, rows_of(part, places) + sender_part(places, send, table, w_in))

    Tiles(counts, (0,), cap, 0, kinds).run(step, 4)


def early_kernel(
    counts, send, recv, src1, w_in, part,
    u_all, rs_all, hidden_all, total,
    source, held,
):
    total[...] = jnp.zeros_like(total)
    hidden_all[hidden_all.shape[0] - 1] = jnp.zeros(hidden_all.shape[1:], bf16)
    source[0] = folded(src1[...])
    cap = send.shape[1]
    results = (u_all, rs_all, hidden_all, total)
    forward(Tiles(counts, (0,), cap, 0, 2), send, recv, None, w_in, part, held, *results)
    forward(Tiles(counts, (1,), cap, 0, 2), send, recv, source, w_in, part, held, *results)


def both_halves(x, axis):
    return jnp.concatenate(halves(x), axis=axis)


def backward(
    tiles, send, recv, edges, grad_edge, w_out, inc_grad, u_all, rs_all, hidden_all,
    held, edge_back, recv_sum, send_sum, edge_turned, out_sum,
):
    nodes = inc_grad.shape[0] * FOLD
    d = w_out.shape[0]

    def front(places):
        picked = Slots(slots_of(recv, places), nodes).rows(inc_grad[...])
        live = live_of(places, d)
        grad_rows = rows_of(grad_edge, places).astype(f32)
        message_grad = jnp.where(live, grad_rows + picked, 0.0).astype(bf16)
        hidden_grad = dot_nt(message_grad, w_out[...])
        u = own_rows_of(u_all, places)
        pre_grad = normed_back(u, own_rows_of(rs_all, places), gate(u), hidden_grad)
        pre_grad = jnp.where(live, pre_grad, 0.0)
        store_rows(edge_back, places, pre_grad.astype(bf16))
        hidden = jnp.concatenate([hidden_all[p.tile] for p in places], axis=1)
        out_sum[...] += dot(hidden, message_grad)
        return pre_grad.T

    def back(places, pre_grad):
        recv_sum[...] += Slots(slots_of(recv, places), nodes).sums(pre_grad)
        edge_turned[...] += dot(pre_grad.astype(bf16), rows_of(edges, places))
        for i, p in enumerate(places):
            part_grad = pre_grad[:, i * SPAN : (i + 1) * SPAN]
            send_sum[p.at] += Slots(p.slots(send), nodes).sums(part_grad)

    tiles.pipelined(front, back, held, BACKWARD)


def senders_back(send_sum, w_in):
    d = w_in.shape[1]
    w_send = jnp.concatenate([w_in[:d, :], w_in[:d, :]], axis=1)
    return dot(w_send, both_halves(unfolded_sums(send_sum), 0)).T.astype(bf16)


def turned_product(sums, table):
    both = dot(both_halves(unfolded_sums(sums), 0), table)
    d = table.shape[1]
    return both[:d] + both[d:]


def node_kernel(
    counts, send, recv, hit, src2, src3, edges, grad_hit, grad_edge,
    w_in, w_out, wn_in, wn_out, part, total_in, odd,
    far_back, near_back, edge_back, recv_sum, node_back, inc_grad, partial,
    source, send_sum, u_all, rs_all, hidden_all, total, held, held_back,
):
    nodes, d = hit.shape
    cap = send.shape[1]
    near = cap // SPAN
    hidden_all[2 * near] = jnp.zeros(hidden_all.shape[1:], bf16)
    total[...] = total_in[...]
    source[0] = folded(src2[...])
    source[1] = folded(src3[...])
    results = (u_all, rs_all, hidden_all, total)
    forward(Tiles(counts, (2, 3), cap, 2, 2), send, recv, source, w_in, part, held, *results)
    upper, lower = halves(unfolded_sums(total[...]).T)
    incoming = (dot(upper, w_out[...]) + dot(lower, w_out[...])).astype(bf16)
    u, rstd = normed(dot(hit[...], wn_in[:d, :]) + dot(incoming, wn_in[d:, :]))
    sig = gate(u)
    hidden = (u * sig).astype(bf16)
    hidden_grad = dot_nt(grad_hit[...], wn_out[...])
    pre_grad = normed_back(u, rstd, sig, hidden_grad).astype(bf16)
    node_back[...] = pre_grad
    inc_grad[...] = folded(dot_nt(pre_grad, wn_in[d:, :]).astype(bf16))
    partial[6 * d : 7 * d, :] = dot_tn(hidden, grad_hit[...])
    partial[4 * d : 5 * d, :] = dot_tn(hit[...], pre_grad)
    partial[5 * d : 6 * d, :] = dot_tn(incoming, pre_grad)
    partial[2 * d : 4 * d, :] = jnp.zeros((2 * d, d), f32)
    recv_sum[...] = jnp.zeros_like(recv_sum)
    send_sum[...] = jnp.zeros_like(send_sum)
    backward(
        Tiles(counts, (2, 3), cap, 2, 2), send, recv, edges, grad_edge, w_out, inc_grad,
        u_all, rs_all, hidden_all, held_back, edge_back, recv_sum, send_sum,
        partial.at[2 * d : 3 * d], partial.at[3 * d : 4 * d],
    )
    partial[:d, :] = turned_product(send_sum[0], src2[...]) + turned_product(send_sum[1], src3[...])
    far_back[...] = senders_back(send_sum[odd[0]], w_in)
    near_back[...] = senders_back(send_sum[1 - odd[0]], w_in)


def last_kernel(
    counts, send, recv, hit, src1, edges, grad_edge, w_in, w_out,
    u0, rs0, hidden0, recv_in, inc_grad, partial, me,
    back1, edge_back, recv_sum, send0, mine, other,
    send_sum, weights, held,
):
    cap, d = send.shape[1], hit.shape[1]
    weights[...] = partial[...]
    recv_sum[...] = recv_in[...]
    send_sum[...] = jnp.zeros_like(send_sum)
    backward(
        Tiles(counts, (0, 1), cap, 0, 2), send, recv, edges, grad_edge, w_out, inc_grad,
        u0, rs0, hidden0, held, edge_back, recv_sum, send_sum,
        weights.at[2 * d : 3 * d], weights.at[3 * d : 4 * d],
    )
    turned = turned_product(send_sum[0], hit[...]) + turned_product(send_sum[1], src1[...])
    weights[:d, :] = (weights[:d, :] + turned).T
    weights[d : 2 * d, :] = turned_product(recv_sum[...], hit[...]).T
    weights[2 * d : 3 * d, :] = weights[2 * d : 3 * d, :].T
    back1[...] = senders_back(send_sum[1], w_in)
    send0[...] = send_sum[0]
    half = mine.shape[0]
    mine[...] = weights[pl.ds(pl.multiple_of(me[0] * half, half), half), :]
    other[...] = weights[pl.ds(pl.multiple_of((1 - me[0]) * half, half), half), :].astype(bf16)


def edge_kernel(
    counts, grad_hit, grad_edge, w_in, wn_in, first_back, second_back, recv_sum, send0, node_back,
    edge_done, hit_done,
):
    d = w_in.shape[1]
    kinds, cap = edge_done.shape[:2]
    for k in range(kinds):
        back = (first_back, second_back)[k // 2][k % 2 * cap : (k % 2 + 1) * cap, :]
        through = dot_nt(back, w_in[2 * d :, :])
        live = lax.broadcasted_iota(jnp.int32, through.shape, 0) < counts[k]
        grad_rows = grad_edge[k * cap : (k + 1) * cap, :].astype(f32)
        edge_done[k] = (grad_rows + jnp.where(live, through, 0.0)).astype(bf16)
    ends = jnp.concatenate([w_in[d : 2 * d, :]] * 2 + [w_in[:d, :]] * 2, axis=1)
    sums = jnp.concatenate([both_halves(unfolded_sums(s[...]), 0) for s in (recv_sum, send0)], axis=0)
    hit_done[...] = (
        grad_hit[...].astype(f32) + dot_nt(node_back[...], wn_in[:d, :]) + dot(ends, sums).T
    )


def closing_kernel(scale, me, mine, theirs, *outs):
    half = mine.shape[0]

    def put(block, start):
        row = 0
        for out in outs:
            low, high = max(row, start), min(row + out.shape[0], start + half)
            if low < high:
                out[low - row : high - row, :] = block[low - start : high - start, :].astype(f32) * scale
            row += out.shape[0]

    @pl.when(me[0] == 0)
    def _():
        put(mine, 0)
        put(theirs, half)

    @pl.when(me[0] != 0)
    def _():
        put(theirs, 0)
        put(mine, half)


def on_device(kernel, outs, operands, flops, scratch=(), scalars=(0,), hbm=False, free=()):
    vmem_spec = pl.BlockSpec(memory_space=pltpu.VMEM)
    smem_spec = pl.BlockSpec(memory_space=pltpu.SMEM)
    in_specs = [smem_spec if i in scalars else vmem_spec for i in range(len(operands))]
    if hbm:
        in_specs = [pl.BlockSpec(memory_space=pltpu.HBM)] * len(operands)
        operands = [pltpu.with_memory_space_constraint(x, pltpu.HBM) for x in operands]
    for i in free:
        in_specs[i] = pl.BlockSpec(memory_space=pl.ANY)
    return pl.pallas_call(
        kernel,
        out_shape=outs,
        in_specs=in_specs,
        out_specs=[vmem_spec] * len(outs),
        scratch_shapes=list(scratch),
        compiler_params=pltpu.CompilerParams(vmem_limit_bytes=VMEM_BYTES),
        cost_estimate=pl.CostEstimate(flops=flops, bytes_accessed=0, transcendentals=0),
    )(*operands)


def summed_over_chips(mine, total, sectors, arrived, finish):
    axes = ("layer", "phi")

    def swap(value, mask):
        return lax.ppermute(value, axes, [(i, i ^ mask) for i in range(total)])

    bits = [1 << b for b in range(total.bit_length() - 1) if 1 << b != sectors]
    near = [1] + [b for b in bits if b > sectors]
    far = [b for b in bits if b not in near]
    ordered = far + near if len(far) % 2 == 0 else near + far
    for at in range(0, len(ordered), 2):
        pair = ordered[at : at + 2]
        masks = pair + [pair[0] ^ pair[1]] if len(pair) == 2 else pair
        sent = mine.astype(bf16)
        mine = sum((swap(sent, m).astype(f32) for m in masks), sent.astype(f32))
        if at == 0:
            mine, arrived = lax.optimization_barrier((mine, arrived))
            beside = finish(arrived)
    mine, beside = lax.optimization_barrier((mine.astype(bf16), beside))
    return mine, swap(mine, sectors), beside


def body(
    hit_features, edge_features, sender_slot, receiver_slot, edge_count, grad_hits, grad_edges,
    w_edge_in, w_edge_out, w_node_in, w_node_out,
):
    hit = hit_features[0, 0]
    nodes, d = hit.shape
    kinds, cap = sender_slot.shape[2:]
    edges, grad_edge = edge_features.reshape(kinds * cap, d), grad_edges.reshape(kinds * cap, d)
    send, recv, counts = sender_slot[0, 0], receiver_slot[0, 0], edge_count[0, 0]
    grad_hit = grad_hits[0, 0]
    layers, sectors = lax.axis_size("layer"), lax.axis_size("phi")
    devices = layers * sectors
    me = (lax.axis_index("layer") % 2).astype(jnp.int32).reshape(1)
    odd = (lax.axis_index("phi") % 2).astype(jnp.int32).reshape(1)
    src2 = shifted(hit, "phi", 1, True)
    src3 = shifted(hit, "phi", -1, True)
    src1 = shifted(hit, "layer", 1, False)

    def shape(*dims, dtype=f32):
        return jax.ShapeDtypeStruct(dims, dtype)

    def rows(count):
        return shape(count * cap + SPAN, d)

    def tiles(count):
        return shape(count * cap // SPAN + 1, d, SPAN, dtype=bf16)

    turned = shape(FOLD * d, nodes // FOLD)
    node_half = shape(nodes, d, dtype=bf16)
    (part,) = on_device(
        local_kernel,
        [rows(kinds)],
        (counts, send, recv, hit, edges, w_edge_in),
        4 * 10**9,
        scratch=[
            pltpu.SMEM(counts.shape, jnp.int32),
            pltpu.VMEM(send.shape, jnp.int32),
            pltpu.VMEM(recv.shape, jnp.int32),
            pltpu.VMEM((nodes, d), bf16),
            pltpu.VMEM(edges.shape, bf16),
            pltpu.VMEM(w_edge_in.shape, bf16),
            pltpu.VMEM((1, nodes // FOLD, FOLD * d), bf16),
            pltpu.SemaphoreType.DMA((6,)),
        ],
        hbm=True,
    )
    u0, rs0, hidden0, total = on_device(
        early_kernel,
        [rows(2), rows(2), tiles(2), turned],
        (counts, send, recv, src1, w_edge_in, part),
        2 * 10**9,
        scratch=[
            pltpu.VMEM((1, nodes // FOLD, FOLD * d), bf16),
            pltpu.VMEM((d, FORWARD * SPAN), f32),
        ],
    )
    partial = shape(7 * d, d)
    far_back, near_back, second_back, recv_sum, node_back, inc_grad, partial = on_device(
        node_kernel,
        [
            node_half, node_half, shape(2 * cap + SPAN, d, dtype=bf16),
            turned, node_half, shape(nodes // FOLD, FOLD * d, dtype=bf16), partial,
        ],
        (counts, send, recv, hit, src2, src3, edges, grad_hit, grad_edge,
         w_edge_in, w_edge_out, w_node_in, w_node_out, part, total, odd),
        8 * 10**9,
        scratch=[
            pltpu.VMEM((2, nodes // FOLD, FOLD * d), bf16),
            pltpu.VMEM((2, *turned.shape), f32),
            pltpu.VMEM((2 * cap + SPAN, d), f32),
            pltpu.VMEM((2 * cap + SPAN, d), f32),
            pltpu.VMEM((2 * cap // SPAN + 1, d, SPAN), bf16),
            pltpu.VMEM(turned.shape, f32),
            pltpu.VMEM((d, FORWARD * SPAN), f32),
            pltpu.VMEM((d, BACKWARD * SPAN), f32),
        ],
        scalars=(0, 15),
    )
    route = [(i, (i + (2 if i % 2 else -2)) % sectors) for i in range(sectors)]
    relayed = lax.ppermute(far_back, "phi", route)
    back1, first_back, recv_sum, send0, mine, other = on_device(
        last_kernel,
        [
            node_half, shape(2 * cap + SPAN, d, dtype=bf16), turned, turned,
            shape(7 * d // 2, d), shape(7 * d // 2, d, dtype=bf16),
        ],
        (counts, send, recv, hit, src1, edges, grad_edge, w_edge_in, w_edge_out,
         u0, rs0, hidden0, recv_sum, inc_grad, partial, me),
        8 * 10**9,
        scratch=[
            pltpu.VMEM((2, *turned.shape), f32),
            pltpu.VMEM((7 * d, d), f32),
            pltpu.VMEM((d, BACKWARD * SPAN), f32),
        ],
        scalars=(0, 15),
    )
    other, relayed = lax.optimization_barrier((other, relayed))
    from_beside = lax.ppermute(
        (near_back.astype(f32) + relayed.astype(f32)).astype(bf16),
        "phi",
        [(i, i ^ 1) for i in range(sectors)],
    )
    mine = mine + lax.ppermute(other, "layer", [(i, i ^ 1) for i in range(layers)]).astype(f32)
    edge_done, hit_done = on_device(
        edge_kernel,
        [shape(kinds, cap, d, dtype=bf16), shape(nodes, d)],
        (counts, grad_hit, grad_edge, w_edge_in, w_node_in,
         first_back, second_back, recv_sum, send0, node_back),
        10**6,
    )
    hit_done, back1 = lax.optimization_barrier((hit_done, back1))
    from_upper = shifted(back1, "layer", -1, False)

    def hits(from_beside):
        return hit_done + from_upper.astype(f32) + from_beside.astype(f32)

    mine, theirs, hit_total = summed_over_chips(mine, devices, sectors, from_beside, hits)
    summed = on_device(
        functools.partial(closing_kernel, 1.0 / devices),
        [shape(3 * d, d), shape(d, d), shape(2 * d, d), shape(d, d)],
        (me, mine, theirs),
        10**6,
    )
    return (hit_total[None, None], edge_done[None, None], *summed)


def solution(mesh):
    placed = (
        P("layer", "phi", None, None),
        P("layer", "phi", None, None, None),
        P("layer", "phi", None, None),
        P("layer", "phi", None, None),
        P("layer", "phi", None),
        P("layer", "phi", None, None),
        P("layer", "phi", None, None, None),
        P(),
        P(),
        P(),
        P(),
    )
    return jax.shard_map(
        body,
        mesh=mesh,
        in_specs=placed,
        out_specs=(
            P("layer", "phi", None, None),
            P("layer", "phi", None, None, None),
            P(),
            P(),
            P(),
            P(),
        ),
        check_vma=False,
    )
```

```python
import functools

import jax
import jax.numpy as jnp
from jax import lax
from jax.experimental import pallas as pl
from jax.experimental.pallas import tpu as pltpu
from jax.sharding import PartitionSpec as P

norm_eps = 1e-05
bf16, f32 = jnp.bfloat16, jnp.float32
SPAN = 256
FOLD = 4
FORWARD = 2
BACKWARD = 2
VMEM_BYTES = 16 * 1024 * 1024


def shifted(value, axis, steps, ring):
    count = lax.axis_size(axis)
    if ring:
        route = [(i, (i + steps) % count) for i in range(count)]
    else:
        route = [(i, i + steps) for i in range(count) if 0 <= i + steps < count]
    return lax.ppermute(value, axis, route)


def dot(a, b):
    return jnp.dot(a, b, preferred_element_type=f32)


def dot_nt(a, b):
    return lax.dot_general(a, b, (((1,), (1,)), ((), ())), preferred_element_type=f32)


def dot_tn(a, b):
    return lax.dot_general(a, b, (((0,), (0,)), ((), ())), preferred_element_type=f32)


def halves(x):
    upper = x.astype(bf16)
    return upper, (x - upper.astype(f32)).astype(bf16)


def folded(table):
    width = table.shape[0] // FOLD
    return jnp.concatenate([table[f * width : (f + 1) * width] for f in range(FOLD)], axis=1)


def unfolded_sums(sums):
    d = sums.shape[0] // FOLD
    return jnp.concatenate([sums[f * d : (f + 1) * d] for f in range(FOLD)], axis=1)


class Slots:
    def __init__(self, idx_row, nodes):
        edges = idx_row.shape[1]
        chunks = nodes // FOLD // 128
        block = idx_row >> 7
        self.part = block // chunks
        low = jnp.broadcast_to((idx_row & 127).astype(f32).astype(bf16), (128, edges)).T
        chunk = (block - self.part * chunks).astype(f32).astype(bf16)
        chunk = jnp.broadcast_to(chunk, (128, edges)).T
        self.part_rows = jnp.broadcast_to(self.part.astype(f32), (128, edges)).T
        lane = lax.broadcasted_iota(jnp.int32, (edges, 128), 1).astype(f32).astype(bf16)
        one = jnp.where(low == lane, bf16(1), bf16(0))
        hots = [jnp.where(chunk == bf16(c), one, bf16(0)) for c in range(chunks)]
        self.hot = jnp.concatenate(hots, axis=1)

    def rows(self, table):
        wide = dot(self.hot, table)
        d = wide.shape[1] // FOLD
        out = wide[:, :d]
        for f in range(1, FOLD):
            out = jnp.where(self.part_rows == f, wide[:, f * d : (f + 1) * d], out)
        return out

    def sums(self, turned):
        parts = [jnp.where(self.part == f, turned, 0.0).astype(bf16) for f in range(FOLD)]
        return dot(jnp.concatenate(parts, axis=0), self.hot)


def normed(pre):
    centred = pre - jnp.mean(pre, axis=-1, keepdims=True)
    rstd = lax.rsqrt(jnp.mean(centred * centred, axis=-1, keepdims=True) + norm_eps)
    return centred * rstd, rstd


def gate(u):
    return 1.0 / (1.0 + jnp.exp(-u))


def normed_back(u, rstd, sig, upstream):
    du = upstream * (sig * (1.0 + u * (1.0 - sig)))
    mean_du = jnp.mean(du, axis=-1, keepdims=True)
    mean_duu = jnp.mean(du * u, axis=-1, keepdims=True)
    return rstd * (du - mean_du - u * mean_duu)


class Tiles:
    def __init__(self, counts, kinds, cap, first, held):
        self.kinds, self.cap, self.first, self.held = kinds, cap, first, held
        self.counts = [counts[k] for k in kinds]
        self.ends = []
        end = jnp.int32(0)
        for count in self.counts:
            end = end + (count + SPAN - 1) // SPAN
            self.ends.append(end)

    def place(self, t):
        kind, at, start, count = self.kinds[0], jnp.int32(0), jnp.int32(0), self.counts[0]
        for i in range(1, len(self.kinds)):
            past = t >= self.ends[i - 1]
            kind = jnp.where(past, self.kinds[i], kind)
            at = jnp.where(past, i, at)
            start = jnp.where(past, self.ends[i - 1], start)
            count = jnp.where(past, self.counts[i], count)
        real = t < self.ends[-1]
        offset = jnp.where(real, (t - start) * SPAN, 0)
        rest = jnp.where(real, count - offset, 0)
        row = kind * self.cap + offset
        store = jnp.where(real, row - self.first * self.cap, self.held * self.cap)
        return Place(kind, at, offset, rest, row, row - self.first * self.cap, store)

    def pipelined(self, front, back, held, group):
        steps = (self.ends[-1] + group - 1) // group

        def places(i):
            return [self.place(group * i + j) for j in range(group)]

        def looped(i, carry):
            back(places(i - 1), held[...])
            held[...] = front(places(i))
            return carry

        @pl.when(steps > 0)
        def _():
            held[...] = front(places(0))
            lax.fori_loop(1, steps, looped, 0)
            back(places(steps - 1), held[...])

    def run(self, step, group=2):
        def looped(i, carry):
            step([self.place(group * i + j) for j in range(group)])
            return carry

        lax.fori_loop(0, (self.ends[-1] + group - 1) // group, looped, 0)


class Place:
    def __init__(self, kind, at, offset, rest, row, own, store):
        self.kind, self.at, self.rest = kind, at, rest
        self.offset = pl.multiple_of(offset, SPAN)
        self.rows = pl.ds(pl.multiple_of(row, SPAN), SPAN)
        self.own = pl.ds(pl.multiple_of(own, SPAN), SPAN)
        self.stored = pl.ds(pl.multiple_of(store, SPAN), SPAN)
        self.tile = store // SPAN

    def slots(self, ref):
        return ref[pl.ds(self.kind, 1), pl.ds(self.offset, SPAN)]


def rows_of(ref, places):
    return jnp.concatenate([ref[p.rows, :] for p in places], axis=0)


def own_rows_of(ref, places):
    return jnp.concatenate([ref[p.own, :] for p in places], axis=0)


def slots_of(ref, places):
    return jnp.concatenate([p.slots(ref) for p in places], axis=1)


def live_of(places, d):
    place = lax.broadcasted_iota(jnp.int32, (SPAN, d), 0)
    return jnp.concatenate([place < p.rest for p in places], axis=0)


def store_rows(ref, places, value):
    for i, p in enumerate(places):
        ref[p.stored, :] = value[i * SPAN : (i + 1) * SPAN]


def receiver_forward(tiles, recv, table, edges, w_in, part):
    nodes, d = table.shape[0] * FOLD, w_in.shape[1]

    def step(places):
        picked = Slots(slots_of(recv, places), nodes).rows(table[...]).astype(bf16)
        pre = dot(picked, w_in[d : 2 * d, :]) + dot(rows_of(edges, places), w_in[2 * d :, :])
        store_rows(part, places, pre)

    tiles.run(step, 4)


def sender_part(places, send, source, w_in):
    nodes, d = source.shape[1] * FOLD, w_in.shape[1]
    picked = [Slots(p.slots(send), nodes).rows(source[p.at]) for p in places]
    return dot(jnp.concatenate(picked, axis=0).astype(bf16), w_in[:d, :])


def forward(tiles, send, recv, source, w_in, part, held, u_all, rs_all, hidden_all, total):
    d = w_in.shape[1]
    nodes = total.shape[1] * FOLD

    def front(places):
        pre = rows_of(part, places)
        if source is not None:
            pre += sender_part(places, send, source, w_in)
        u, rstd = normed(pre)
        store_rows(u_all, places, u)
        store_rows(rs_all, places, jnp.broadcast_to(rstd, u.shape))
        hidden = jnp.where(live_of(places, d), u * gate(u), 0.0).T
        for i, p in enumerate(places):
            hidden_all[p.tile] = hidden[:, i * SPAN : (i + 1) * SPAN].astype(bf16)
        return hidden

    def back(places, hidden):
        total[...] += Slots(slots_of(recv, places), nodes).sums(hidden)

    tiles.pipelined(front, back, held, FORWARD)


def local_kernel(
    counts_far, send_far, recv_far, hit_far, edges_far, w_in_far,
    part,
    counts, send, recv, hit, edges, w_in, table, arrived,
):
    far = (counts_far, send_far, recv_far, hit_far, edges_far, w_in_far)
    near = (counts, send, recv, hit, edges, w_in)
    copies = [pltpu.make_async_copy(f, n, arrived.at[i]) for i, (f, n) in enumerate(zip(far, near))]
    for copy in copies:
        copy.start()
    for copy in copies:
        copy.wait()
    table[0] = folded(hit[...])
    kinds, cap = send.shape
    tiles = Tiles(counts, tuple(range(kinds)), cap, 0, kinds)
    receiver_forward(tiles, recv, table.at[0], edges, w_in, part)

    def step(places):
        store_rows(part, places, rows_of(part, places) + sender_part(places, send, table, w_in))

    Tiles(counts, (0,), cap, 0, kinds).run(step, 4)


def early_kernel(
    counts, send, recv, src1, w_in, part,
    u_all, rs_all, hidden_all, total,
    source, held,
):
    total[...] = jnp.zeros_like(total)
    hidden_all[hidden_all.shape[0] - 1] = jnp.zeros(hidden_all.shape[1:], bf16)
    source[0] = folded(src1[...])
    cap = send.shape[1]
    results = (u_all, rs_all, hidden_all, total)
    forward(Tiles(counts, (0,), cap, 0, 2), send, recv, None, w_in, part, held, *results)
    forward(Tiles(counts, (1,), cap, 0, 2), send, recv, source, w_in, part, held, *results)


def both_halves(x, axis):
    return jnp.concatenate(halves(x), axis=axis)


def backward(
    tiles, send, recv, edges, grad_edge, w_out, inc_grad, u_all, rs_all, hidden_all,
    held, edge_back, recv_sum, send_sum, edge_turned, out_sum,
):
    nodes = inc_grad.shape[0] * FOLD
    d = w_out.shape[0]

    def front(places):
        picked = Slots(slots_of(recv, places), nodes).rows(inc_grad[...])
        live = live_of(places, d)
        grad_rows = rows_of(grad_edge, places).astype(f32)
        message_grad = jnp.where(live, grad_rows + picked, 0.0).astype(bf16)
        hidden_grad = dot_nt(message_grad, w_out[...])
        u = own_rows_of(u_all, places)
        pre_grad = normed_back(u, own_rows_of(rs_all, places), gate(u), hidden_grad)
        pre_grad = jnp.where(live, pre_grad, 0.0)
        store_rows(edge_back, places, pre_grad.astype(bf16))
        hidden = jnp.concatenate([hidden_all[p.tile] for p in places], axis=1)
        out_sum[...] += dot(hidden, message_grad)
        return pre_grad.T

    def back(places, pre_grad):
        recv_sum[...] += Slots(slots_of(recv, places), nodes).sums(pre_grad)
        edge_turned[...] += dot(pre_grad.astype(bf16), rows_of(edges, places))
        for i, p in enumerate(places):
            part_grad = pre_grad[:, i * SPAN : (i + 1) * SPAN]
            send_sum[p.at] += Slots(p.slots(send), nodes).sums(part_grad)

    tiles.pipelined(front, back, held, BACKWARD)


def senders_back(send_sum, w_in):
    d = w_in.shape[1]
    w_send = jnp.concatenate([w_in[:d, :], w_in[:d, :]], axis=1)
    return dot(w_send, both_halves(unfolded_sums(send_sum), 0)).T.astype(bf16)


def turned_product(sums, table):
    both = dot(both_halves(unfolded_sums(sums), 0), table)
    d = table.shape[1]
    return both[:d] + both[d:]


def node_kernel(
    counts, send, recv, hit, src2, src3, edges, grad_hit, grad_edge,
    w_in, w_out, wn_in, wn_out, part, total_in, odd,
    far_back, edge_back, recv_sum, node_back, inc_grad, partial, u_all, rs_all, hidden_all,
    source, send_sum, total, held, held_back,
):
    nodes, d = hit.shape
    cap = send.shape[1]
    near = cap // SPAN
    hidden_all[2 * near] = jnp.zeros(hidden_all.shape[1:], bf16)
    total[...] = total_in[...]
    source[0] = folded(src2[...])
    source[1] = folded(src3[...])
    results = (u_all, rs_all, hidden_all, total)
    forward(Tiles(counts, (2, 3), cap, 2, 2), send, recv, source, w_in, part, held, *results)
    upper, lower = halves(unfolded_sums(total[...]).T)
    incoming = (dot(upper, w_out[...]) + dot(lower, w_out[...])).astype(bf16)
    u, rstd = normed(dot(hit[...], wn_in[:d, :]) + dot(incoming, wn_in[d:, :]))
    sig = gate(u)
    hidden = (u * sig).astype(bf16)
    hidden_grad = dot_nt(grad_hit[...], wn_out[...])
    pre_grad = normed_back(u, rstd, sig, hidden_grad).astype(bf16)
    node_back[...] = pre_grad
    inc_grad[...] = folded(dot_nt(pre_grad, wn_in[d:, :]).astype(bf16))
    partial[6 * d : 7 * d, :] = dot_tn(hidden, grad_hit[...])
    partial[4 * d : 5 * d, :] = dot_tn(hit[...], pre_grad)
    partial[5 * d : 6 * d, :] = dot_tn(incoming, pre_grad)
    partial[2 * d : 4 * d, :] = jnp.zeros((2 * d, d), f32)
    recv_sum[...] = jnp.zeros_like(recv_sum)
    send_sum[...] = jnp.zeros_like(send_sum)
    backward(
        Tiles(counts, (2 + odd[0],), cap, 2, 2), send, recv, edges, grad_edge, w_out, inc_grad,
        u_all, rs_all, hidden_all, held_back, edge_back, recv_sum, send_sum,
        partial.at[2 * d : 3 * d], partial.at[3 * d : 4 * d],
    )
    far = jnp.where(odd[0] == 1, src3[...].astype(f32), src2[...].astype(f32)).astype(bf16)
    partial[:d, :] = turned_product(send_sum[0], far)
    far_back[...] = senders_back(send_sum[0], w_in)


def last_kernel(
    counts, send, recv, hit, src1, src2, src3, edges, grad_edge, w_in, w_out,
    u0, rs0, hidden0, u2, rs2, hidden2, recv_in, inc_grad, partial, me, odd,
    back1, near_back, edge_back, near_edge, recv_sum, send0, mine, other,
    send_sum, weights, held,
):
    cap, d = send.shape[1], hit.shape[1]
    weights[...] = partial[...]
    recv_sum[...] = recv_in[...]
    send_sum[...] = jnp.zeros_like(send_sum)
    backward(
        Tiles(counts, (0, 1), cap, 0, 2), send, recv, edges, grad_edge, w_out, inc_grad,
        u0, rs0, hidden0, held, edge_back, recv_sum, send_sum,
        weights.at[2 * d : 3 * d], weights.at[3 * d : 4 * d],
    )
    backward(
        Tiles(counts, (3 - odd[0],), cap, 2, 2), send, recv, edges, grad_edge, w_out, inc_grad,
        u2, rs2, hidden2, held, near_edge, recv_sum, send_sum.at[2:],
        weights.at[2 * d : 3 * d], weights.at[3 * d : 4 * d],
    )
    near = jnp.where(odd[0] == 1, src2[...].astype(f32), src3[...].astype(f32)).astype(bf16)
    near_back[...] = senders_back(send_sum[2], w_in)
    turned = turned_product(send_sum[0], hit[...]) + turned_product(send_sum[1], src1[...])
    turned += turned_product(send_sum[2], near)
    weights[:d, :] = (weights[:d, :] + turned).T
    weights[d : 2 * d, :] = turned_product(recv_sum[...], hit[...]).T
    weights[2 * d : 3 * d, :] = weights[2 * d : 3 * d, :].T
    back1[...] = senders_back(send_sum[1], w_in)
    send0[...] = send_sum[0]
    half = mine.shape[0]
    mine[...] = weights[pl.ds(pl.multiple_of(me[0] * half, half), half), :]
    other[...] = weights[pl.ds(pl.multiple_of((1 - me[0]) * half, half), half), :].astype(bf16)


def edge_kernel(
    counts, grad_hit, grad_edge, w_in, wn_in, first_back, far_edge, near_edge, recv_sum, send0, node_back, odd,
    edge_done, hit_done,
):
    d = w_in.shape[1]
    cap = edge_done.shape[1]

    def put(kind, back, row):
        through = dot_nt(back[pl.ds(row * cap, cap), :], w_in[2 * d :, :])
        live = lax.broadcasted_iota(jnp.int32, through.shape, 0) < counts[kind]
        grad_rows = grad_edge[pl.ds(kind * cap, cap), :].astype(f32)
        edge_done[kind] = (grad_rows + jnp.where(live, through, 0.0)).astype(bf16)

    put(0, first_back, 0)
    put(1, first_back, 1)
    put(2 + odd[0], far_edge, odd[0])
    put(3 - odd[0], near_edge, 1 - odd[0])
    ends = jnp.concatenate([w_in[d : 2 * d, :]] * 2 + [w_in[:d, :]] * 2, axis=1)
    sums = jnp.concatenate([both_halves(unfolded_sums(s[...]), 0) for s in (recv_sum, send0)], axis=0)
    hit_done[...] = (
        grad_hit[...].astype(f32) + dot_nt(node_back[...], wn_in[:d, :]) + dot(ends, sums).T
    )


def closing_kernel(scale, me, mine, theirs, *outs):
    half = mine.shape[0]

    def put(block, start):
        row = 0
        for out in outs:
            low, high = max(row, start), min(row + out.shape[0], start + half)
            if low < high:
                out[low - row : high - row, :] = block[low - start : high - start, :].astype(f32) * scale
            row += out.shape[0]

    @pl.when(me[0] == 0)
    def _():
        put(mine, 0)
        put(theirs, half)

    @pl.when(me[0] != 0)
    def _():
        put(theirs, 0)
        put(mine, half)


def on_device(kernel, outs, operands, flops, scratch=(), scalars=(0,), hbm=False, free=()):
    vmem_spec = pl.BlockSpec(memory_space=pltpu.VMEM)
    smem_spec = pl.BlockSpec(memory_space=pltpu.SMEM)
    in_specs = [smem_spec if i in scalars else vmem_spec for i in range(len(operands))]
    if hbm:
        in_specs = [pl.BlockSpec(memory_space=pltpu.HBM)] * len(operands)
        operands = [pltpu.with_memory_space_constraint(x, pltpu.HBM) for x in operands]
    for i in free:
        in_specs[i] = pl.BlockSpec(memory_space=pl.ANY)
    return pl.pallas_call(
        kernel,
        out_shape=outs,
        in_specs=in_specs,
        out_specs=[vmem_spec] * len(outs),
        scratch_shapes=list(scratch),
        compiler_params=pltpu.CompilerParams(vmem_limit_bytes=VMEM_BYTES),
        cost_estimate=pl.CostEstimate(flops=flops, bytes_accessed=0, transcendentals=0),
    )(*operands)


def summed_over_chips(mine, total, sectors, arrived, finish):
    axes = ("layer", "phi")

    def swap(value, mask):
        return lax.ppermute(value, axes, [(i, i ^ mask) for i in range(total)])

    bits = [1 << b for b in range(total.bit_length() - 1) if 1 << b != sectors]
    near = [1] + [b for b in bits if b > sectors]
    far = [b for b in bits if b not in near]
    ordered = far + near if len(far) % 2 == 0 else near + far
    for at in range(0, len(ordered), 2):
        pair = ordered[at : at + 2]
        masks = pair + [pair[0] ^ pair[1]] if len(pair) == 2 else pair
        sent = mine.astype(bf16)
        mine = sum((swap(sent, m).astype(f32) for m in masks), sent.astype(f32))
        if at == 0:
            mine, arrived = lax.optimization_barrier((mine, arrived))
            beside = finish(arrived)
    mine, beside = lax.optimization_barrier((mine.astype(bf16), beside))
    return mine, swap(mine, sectors), beside


def body(
    hit_features, edge_features, sender_slot, receiver_slot, edge_count, grad_hits, grad_edges,
    w_edge_in, w_edge_out, w_node_in, w_node_out,
):
    hit = hit_features[0, 0]
    nodes, d = hit.shape
    kinds, cap = sender_slot.shape[2:]
    edges, grad_edge = edge_features.reshape(kinds * cap, d), grad_edges.reshape(kinds * cap, d)
    send, recv, counts = sender_slot[0, 0], receiver_slot[0, 0], edge_count[0, 0]
    grad_hit = grad_hits[0, 0]
    layers, sectors = lax.axis_size("layer"), lax.axis_size("phi")
    devices = layers * sectors
    me = (lax.axis_index("layer") % 2).astype(jnp.int32).reshape(1)
    odd = (lax.axis_index("phi") % 2).astype(jnp.int32).reshape(1)
    src2 = shifted(hit, "phi", 1, True)
    src3 = shifted(hit, "phi", -1, True)
    src1 = shifted(lax.optimization_barrier(hit), "layer", 1, False)

    def shape(*dims, dtype=f32):
        return jax.ShapeDtypeStruct(dims, dtype)

    def rows(count):
        return shape(count * cap + SPAN, d)

    def tiles(count):
        return shape(count * cap // SPAN + 1, d, SPAN, dtype=bf16)

    turned = shape(FOLD * d, nodes // FOLD)
    node_half = shape(nodes, d, dtype=bf16)
    (part,) = on_device(
        local_kernel,
        [rows(kinds)],
        (counts, send, recv, hit, edges, w_edge_in),
        4 * 10**9,
        scratch=[
            pltpu.SMEM(counts.shape, jnp.int32),
            pltpu.VMEM(send.shape, jnp.int32),
            pltpu.VMEM(recv.shape, jnp.int32),
            pltpu.VMEM((nodes, d), bf16),
            pltpu.VMEM(edges.shape, bf16),
            pltpu.VMEM(w_edge_in.shape, bf16),
            pltpu.VMEM((1, nodes // FOLD, FOLD * d), bf16),
            pltpu.SemaphoreType.DMA((6,)),
        ],
        hbm=True,
    )
    u0, rs0, hidden0, total = on_device(
        early_kernel,
        [rows(2), rows(2), tiles(2), turned],
        (counts, send, recv, src1, w_edge_in, part),
        2 * 10**9,
        scratch=[
            pltpu.VMEM((1, nodes // FOLD, FOLD * d), bf16),
            pltpu.VMEM((d, FORWARD * SPAN), f32),
        ],
    )
    partial = shape(7 * d, d)
    far_back, far_edge, recv_sum, node_back, inc_grad, partial, u2, rs2, hidden2 = on_device(
        node_kernel,
        [
            node_half, shape(2 * cap + SPAN, d, dtype=bf16),
            turned, node_half, shape(nodes // FOLD, FOLD * d, dtype=bf16), partial,
            rows(2), rows(2), tiles(2),
        ],
        (counts, send, recv, hit, src2, src3, edges, grad_hit, grad_edge,
         w_edge_in, w_edge_out, w_node_in, w_node_out, part, total, odd),
        8 * 10**9,
        scratch=[
            pltpu.VMEM((2, nodes // FOLD, FOLD * d), bf16),
            pltpu.VMEM((1, *turned.shape), f32),
            pltpu.VMEM(turned.shape, f32),
            pltpu.VMEM((d, FORWARD * SPAN), f32),
            pltpu.VMEM((d, BACKWARD * SPAN), f32),
        ],
        scalars=(0, 15),
    )
    route = [(i, (i + (2 if i % 2 else -2)) % sectors) for i in range(sectors)]
    relayed = lax.ppermute(far_back, "phi", route)
    back1, near_back, first_back, near_edge, recv_sum, send0, mine, other = on_device(
        last_kernel,
        [
            node_half, node_half, shape(2 * cap + SPAN, d, dtype=bf16),
            shape(2 * cap + SPAN, d, dtype=bf16), turned, turned,
            shape(7 * d // 2, d), shape(7 * d // 2, d, dtype=bf16),
        ],
        (counts, send, recv, hit, src1, src2, src3, edges, grad_edge, w_edge_in, w_edge_out,
         u0, rs0, hidden0, u2, rs2, hidden2, recv_sum, inc_grad, partial, me, odd),
        8 * 10**9,
        scratch=[
            pltpu.VMEM((3, *turned.shape), f32),
            pltpu.VMEM((7 * d, d), f32),
            pltpu.VMEM((d, BACKWARD * SPAN), f32),
        ],
        scalars=(0, 20, 21),
    )
    other, relayed = lax.optimization_barrier((other, relayed))
    near_back = (near_back.astype(f32) + relayed.astype(f32)).astype(bf16)
    near_back, back1 = lax.optimization_barrier((near_back, back1))
    from_beside = lax.ppermute(near_back, "phi", [(i, i ^ 1) for i in range(sectors)])
    from_upper = shifted(back1, "layer", -1, False)
    mine = mine + lax.ppermute(other, "layer", [(i, i ^ 1) for i in range(layers)]).astype(f32)
    edge_done, hit_done = on_device(
        edge_kernel,
        [shape(kinds, cap, d, dtype=bf16), shape(nodes, d)],
        (counts, grad_hit, grad_edge, w_edge_in, w_node_in,
         first_back, far_edge, near_edge, recv_sum, send0, node_back, odd),
        10**6,
        scalars=(0, 11),
    )

    def hits(from_beside):
        return hit_done + from_upper.astype(f32) + from_beside.astype(f32)

    mine, theirs, hit_total = summed_over_chips(mine, devices, sectors, from_beside, hits)
    summed = on_device(
        functools.partial(closing_kernel, 1.0 / devices),
        [shape(3 * d, d), shape(d, d), shape(2 * d, d), shape(d, d)],
        (me, mine, theirs),
        10**6,
    )
    return (hit_total[None, None], edge_done[None, None], *summed)


def solution(mesh):
    placed = (
        P("layer", "phi", None, None),
        P("layer", "phi", None, None, None),
        P("layer", "phi", None, None),
        P("layer", "phi", None, None),
        P("layer", "phi", None),
        P("layer", "phi", None, None),
        P("layer", "phi", None, None, None),
        P(),
        P(),
        P(),
        P(),
    )
    return jax.shard_map(
        body,
        mesh=mesh,
        in_specs=placed,
        out_specs=(
            P("layer", "phi", None, None),
            P("layer", "phi", None, None, None),
            P(),
            P(),
            P(),
            P(),
        ),
        check_vma=False,
    )
```

```python
import functools

import jax
import jax.numpy as jnp
from jax import lax
from jax.experimental import pallas as pl
from jax.experimental.pallas import tpu as pltpu
from jax.sharding import PartitionSpec as P

norm_eps = 1e-05
bf16, f32 = jnp.bfloat16, jnp.float32
SPAN = 256
FOLD = 4
FORWARD = 2
BACKWARD = 2
VMEM_BYTES = 16 * 1024 * 1024


def shifted(value, axis, steps, ring):
    count = lax.axis_size(axis)
    if ring:
        route = [(i, (i + steps) % count) for i in range(count)]
    else:
        route = [(i, i + steps) for i in range(count) if 0 <= i + steps < count]
    return lax.ppermute(value, axis, route)


def dot(a, b):
    return jnp.dot(a, b, preferred_element_type=f32)


def dot_nt(a, b):
    return lax.dot_general(a, b, (((1,), (1,)), ((), ())), preferred_element_type=f32)


def dot_tn(a, b):
    return lax.dot_general(a, b, (((0,), (0,)), ((), ())), preferred_element_type=f32)


def halves(x):
    upper = x.astype(bf16)
    return upper, (x - upper.astype(f32)).astype(bf16)


def folded(table):
    width = table.shape[0] // FOLD
    return jnp.concatenate([table[f * width : (f + 1) * width] for f in range(FOLD)], axis=1)


def unfolded_sums(sums):
    d = sums.shape[0] // FOLD
    return jnp.concatenate([sums[f * d : (f + 1) * d] for f in range(FOLD)], axis=1)


class Slots:
    def __init__(self, idx_row, nodes):
        edges = idx_row.shape[1]
        chunks = nodes // FOLD // 128
        block = idx_row >> 7
        self.part = block // chunks
        low = jnp.broadcast_to((idx_row & 127).astype(f32).astype(bf16), (128, edges)).T
        chunk = (block - self.part * chunks).astype(f32).astype(bf16)
        chunk = jnp.broadcast_to(chunk, (128, edges)).T
        self.part_rows = jnp.broadcast_to(self.part.astype(f32), (128, edges)).T
        lane = lax.broadcasted_iota(jnp.int32, (edges, 128), 1).astype(f32).astype(bf16)
        one = jnp.where(low == lane, bf16(1), bf16(0))
        hots = [jnp.where(chunk == bf16(c), one, bf16(0)) for c in range(chunks)]
        self.hot = jnp.concatenate(hots, axis=1)

    def rows(self, table):
        wide = dot(self.hot, table)
        d = wide.shape[1] // FOLD
        out = wide[:, :d]
        for f in range(1, FOLD):
            out = jnp.where(self.part_rows == f, wide[:, f * d : (f + 1) * d], out)
        return out

    def sums(self, turned):
        parts = [jnp.where(self.part == f, turned, 0.0).astype(bf16) for f in range(FOLD)]
        return dot(jnp.concatenate(parts, axis=0), self.hot)


def normed(pre):
    centred = pre - jnp.mean(pre, axis=-1, keepdims=True)
    rstd = lax.rsqrt(jnp.mean(centred * centred, axis=-1, keepdims=True) + norm_eps)
    return centred * rstd, rstd


def gate(u):
    return 1.0 / (1.0 + jnp.exp(-u))


def normed_back(u, rstd, sig, upstream):
    du = upstream * (sig * (1.0 + u * (1.0 - sig)))
    mean_du = jnp.mean(du, axis=-1, keepdims=True)
    mean_duu = jnp.mean(du * u, axis=-1, keepdims=True)
    return rstd * (du - mean_du - u * mean_duu)


class Tiles:
    def __init__(self, counts, kinds, cap, first, held):
        self.kinds, self.cap, self.first, self.held = kinds, cap, first, held
        self.counts = [counts[k] for k in kinds]
        self.ends = []
        end = jnp.int32(0)
        for count in self.counts:
            end = end + (count + SPAN - 1) // SPAN
            self.ends.append(end)

    def place(self, t):
        kind, at, start, count = self.kinds[0], jnp.int32(0), jnp.int32(0), self.counts[0]
        for i in range(1, len(self.kinds)):
            past = t >= self.ends[i - 1]
            kind = jnp.where(past, self.kinds[i], kind)
            at = jnp.where(past, i, at)
            start = jnp.where(past, self.ends[i - 1], start)
            count = jnp.where(past, self.counts[i], count)
        real = t < self.ends[-1]
        offset = jnp.where(real, (t - start) * SPAN, 0)
        rest = jnp.where(real, count - offset, 0)
        row = kind * self.cap + offset
        store = jnp.where(real, row - self.first * self.cap, self.held * self.cap)
        return Place(kind, at, offset, rest, row, row - self.first * self.cap, store)

    def pipelined(self, front, back, held, group):
        steps = (self.ends[-1] + group - 1) // group

        def places(i):
            return [self.place(group * i + j) for j in range(group)]

        def looped(i, carry):
            back(places(i - 1), held[...])
            held[...] = front(places(i))
            return carry

        @pl.when(steps > 0)
        def _():
            held[...] = front(places(0))
            lax.fori_loop(1, steps, looped, 0)
            back(places(steps - 1), held[...])

    def run(self, step, group=2):
        def looped(i, carry):
            step([self.place(group * i + j) for j in range(group)])
            return carry

        lax.fori_loop(0, (self.ends[-1] + group - 1) // group, looped, 0)


class Place:
    def __init__(self, kind, at, offset, rest, row, own, store):
        self.kind, self.at, self.rest = kind, at, rest
        self.offset = pl.multiple_of(offset, SPAN)
        self.rows = pl.ds(pl.multiple_of(row, SPAN), SPAN)
        self.own = pl.ds(pl.multiple_of(own, SPAN), SPAN)
        self.stored = pl.ds(pl.multiple_of(store, SPAN), SPAN)
        self.tile = store // SPAN

    def slots(self, ref):
        return ref[pl.ds(self.kind, 1), pl.ds(self.offset, SPAN)]


def rows_of(ref, places):
    return jnp.concatenate([ref[p.rows, :] for p in places], axis=0)


def own_rows_of(ref, places):
    return jnp.concatenate([ref[p.own, :] for p in places], axis=0)


def slots_of(ref, places):
    return jnp.concatenate([p.slots(ref) for p in places], axis=1)


def live_of(places, d):
    place = lax.broadcasted_iota(jnp.int32, (SPAN, d), 0)
    return jnp.concatenate([place < p.rest for p in places], axis=0)


def store_rows(ref, places, value):
    for i, p in enumerate(places):
        ref[p.stored, :] = value[i * SPAN : (i + 1) * SPAN]


def receiver_forward(tiles, recv, table, edges, w_in, part):
    nodes, d = table.shape[0] * FOLD, w_in.shape[1]

    def step(places):
        picked = Slots(slots_of(recv, places), nodes).rows(table[...]).astype(bf16)
        pre = dot(picked, w_in[d : 2 * d, :]) + dot(rows_of(edges, places), w_in[2 * d :, :])
        store_rows(part, places, pre)

    tiles.run(step, 4)


def sender_part(places, send, source, w_in):
    nodes, d = source.shape[1] * FOLD, w_in.shape[1]
    picked = [Slots(p.slots(send), nodes).rows(source[p.at]) for p in places]
    return dot(jnp.concatenate(picked, axis=0).astype(bf16), w_in[:d, :])


def forward(tiles, send, recv, source, w_in, part, held, u_all, rs_all, hidden_all, total):
    d = w_in.shape[1]
    nodes = total.shape[1] * FOLD

    def front(places):
        pre = rows_of(part, places)
        if source is not None:
            pre += sender_part(places, send, source, w_in)
        u, rstd = normed(pre)
        store_rows(u_all, places, u)
        store_rows(rs_all, places, jnp.broadcast_to(rstd, u.shape))
        hidden = jnp.where(live_of(places, d), u * gate(u), 0.0).T
        for i, p in enumerate(places):
            hidden_all[p.tile] = hidden[:, i * SPAN : (i + 1) * SPAN].astype(bf16)
        return hidden

    def back(places, hidden):
        total[...] += Slots(slots_of(recv, places), nodes).sums(hidden)

    tiles.pipelined(front, back, held, FORWARD)


def local_kernel(
    counts_far, send_far, recv_far, hit_far, edges_far, w_in_far,
    part,
    counts, send, recv, hit, edges, w_in, table, arrived,
):
    far = (counts_far, send_far, recv_far, hit_far, edges_far, w_in_far)
    near = (counts, send, recv, hit, edges, w_in)
    copies = [pltpu.make_async_copy(f, n, arrived.at[i]) for i, (f, n) in enumerate(zip(far, near))]
    for copy in copies:
        copy.start()
    for copy in copies:
        copy.wait()
    table[0] = folded(hit[...])
    kinds, cap = send.shape
    tiles = Tiles(counts, tuple(range(kinds)), cap, 0, kinds)
    receiver_forward(tiles, recv, table.at[0], edges, w_in, part)

    def step(places):
        store_rows(part, places, rows_of(part, places) + sender_part(places, send, table, w_in))

    Tiles(counts, (0,), cap, 0, kinds).run(step, 4)


def early_kernel(
    counts, send, recv, src1, w_in, part,
    u_all, rs_all, hidden_all, total,
    source, held,
):
    total[...] = jnp.zeros_like(total)
    hidden_all[hidden_all.shape[0] - 1] = jnp.zeros(hidden_all.shape[1:], bf16)
    source[0] = folded(src1[...])
    cap = send.shape[1]
    results = (u_all, rs_all, hidden_all, total)
    forward(Tiles(counts, (0,), cap, 0, 2), send, recv, None, w_in, part, held, *results)
    forward(Tiles(counts, (1,), cap, 0, 2), send, recv, source, w_in, part, held, *results)


def both_halves(x, axis):
    return jnp.concatenate(halves(x), axis=axis)


def backward(
    tiles, send, recv, edges, grad_edge, w_out, inc_grad, u_all, rs_all, hidden_all,
    held, edge_back, recv_sum, send_sum, edge_turned, out_sum,
):
    nodes = inc_grad.shape[0] * FOLD
    d = w_out.shape[0]

    def front(places):
        picked = Slots(slots_of(recv, places), nodes).rows(inc_grad[...])
        live = live_of(places, d)
        grad_rows = rows_of(grad_edge, places).astype(f32)
        message_grad = jnp.where(live, grad_rows + picked, 0.0).astype(bf16)
        hidden_grad = dot_nt(message_grad, w_out[...])
        u = own_rows_of(u_all, places)
        pre_grad = normed_back(u, own_rows_of(rs_all, places), gate(u), hidden_grad)
        pre_grad = jnp.where(live, pre_grad, 0.0)
        store_rows(edge_back, places, pre_grad.astype(bf16))
        hidden = jnp.concatenate([hidden_all[p.tile] for p in places], axis=1)
        out_sum[...] += dot(hidden, message_grad)
        return pre_grad.T

    def back(places, pre_grad):
        recv_sum[...] += Slots(slots_of(recv, places), nodes).sums(pre_grad)
        edge_turned[...] += dot(pre_grad.astype(bf16), rows_of(edges, places))
        for i, p in enumerate(places):
            part_grad = pre_grad[:, i * SPAN : (i + 1) * SPAN]
            send_sum[p.at] += Slots(p.slots(send), nodes).sums(part_grad)

    tiles.pipelined(front, back, held, BACKWARD)


def senders_back(send_sum, w_in):
    d = w_in.shape[1]
    w_send = jnp.concatenate([w_in[:d, :], w_in[:d, :]], axis=1)
    return dot(w_send, both_halves(unfolded_sums(send_sum), 0)).T.astype(bf16)


def turned_product(sums, table):
    both = dot(both_halves(unfolded_sums(sums), 0), table)
    d = table.shape[1]
    return both[:d] + both[d:]


def node_kernel(
    counts, send, recv, hit, src2, src3, edges, grad_hit, grad_edge,
    w_in, w_out, wn_in, wn_out, part, total_in, odd,
    far_back, edge_back, recv_sum, node_back, inc_grad, partial, u_all, rs_all, hidden_all,
    source, send_sum, total, held, held_back,
):
    nodes, d = hit.shape
    cap = send.shape[1]
    near = cap // SPAN
    hidden_all[2 * near] = jnp.zeros(hidden_all.shape[1:], bf16)
    total[...] = total_in[...]
    source[0] = folded(src2[...])
    source[1] = folded(src3[...])
    results = (u_all, rs_all, hidden_all, total)
    forward(Tiles(counts, (2, 3), cap, 2, 2), send, recv, source, w_in, part, held, *results)
    upper, lower = halves(unfolded_sums(total[...]).T)
    incoming = (dot(upper, w_out[...]) + dot(lower, w_out[...])).astype(bf16)
    u, rstd = normed(dot(hit[...], wn_in[:d, :]) + dot(incoming, wn_in[d:, :]))
    sig = gate(u)
    hidden = (u * sig).astype(bf16)
    hidden_grad = dot_nt(grad_hit[...], wn_out[...])
    pre_grad = normed_back(u, rstd, sig, hidden_grad).astype(bf16)
    node_back[...] = pre_grad
    inc_grad[...] = folded(dot_nt(pre_grad, wn_in[d:, :]).astype(bf16))
    partial[6 * d : 7 * d, :] = dot_tn(hidden, grad_hit[...])
    partial[4 * d : 5 * d, :] = dot_tn(hit[...], pre_grad)
    partial[5 * d : 6 * d, :] = dot_tn(incoming, pre_grad)
    partial[2 * d : 4 * d, :] = jnp.zeros((2 * d, d), f32)
    recv_sum[...] = jnp.zeros_like(recv_sum)
    send_sum[...] = jnp.zeros_like(send_sum)
    backward(
        Tiles(counts, (2 + odd[0],), cap, 2, 2), send, recv, edges, grad_edge, w_out, inc_grad,
        u_all, rs_all, hidden_all, held_back, edge_back, recv_sum, send_sum,
        partial.at[2 * d : 3 * d], partial.at[3 * d : 4 * d],
    )
    far = jnp.where(odd[0] == 1, src3[...].astype(f32), src2[...].astype(f32)).astype(bf16)
    partial[:d, :] = turned_product(send_sum[0], far)
    far_back[...] = senders_back(send_sum[0], w_in)


def last_kernel(
    counts, send, recv, hit, src1, src2, src3, edges, grad_edge, w_in, w_out,
    u0, rs0, hidden0, u2, rs2, hidden2, recv_in, inc_grad, partial, me, odd,
    back1, near_back, edge_back, near_edge, recv_sum, send0, mine, other,
    send_sum, weights, held,
):
    cap, d = send.shape[1], hit.shape[1]
    weights[...] = partial[...]
    recv_sum[...] = recv_in[...]
    send_sum[...] = jnp.zeros_like(send_sum)
    backward(
        Tiles(counts, (0, 1), cap, 0, 2), send, recv, edges, grad_edge, w_out, inc_grad,
        u0, rs0, hidden0, held, edge_back, recv_sum, send_sum,
        weights.at[2 * d : 3 * d], weights.at[3 * d : 4 * d],
    )
    backward(
        Tiles(counts, (3 - odd[0],), cap, 2, 2), send, recv, edges, grad_edge, w_out, inc_grad,
        u2, rs2, hidden2, held, near_edge, recv_sum, send_sum.at[2:],
        weights.at[2 * d : 3 * d], weights.at[3 * d : 4 * d],
    )
    near = jnp.where(odd[0] == 1, src2[...].astype(f32), src3[...].astype(f32)).astype(bf16)
    near_back[...] = senders_back(send_sum[2], w_in)
    turned = turned_product(send_sum[0], hit[...]) + turned_product(send_sum[1], src1[...])
    turned += turned_product(send_sum[2], near)
    weights[:d, :] = (weights[:d, :] + turned).T
    weights[d : 2 * d, :] = turned_product(recv_sum[...], hit[...]).T
    weights[2 * d : 3 * d, :] = weights[2 * d : 3 * d, :].T
    back1[...] = senders_back(send_sum[1], w_in)
    send0[...] = send_sum[0]
    half = mine.shape[0]
    mine[...] = weights[pl.ds(pl.multiple_of(me[0] * half, half), half), :]
    other[...] = weights[pl.ds(pl.multiple_of((1 - me[0]) * half, half), half), :].astype(bf16)


def edge_kernel(
    counts, grad_hit, grad_edge, w_in, wn_in, first_back, far_edge, near_edge, recv_sum, send0, node_back, odd,
    edge_done, hit_done,
):
    d = w_in.shape[1]
    cap = edge_done.shape[1]

    def put(kind, back, row):
        through = dot_nt(back[pl.ds(row * cap, cap), :], w_in[2 * d :, :])
        live = lax.broadcasted_iota(jnp.int32, through.shape, 0) < counts[kind]
        grad_rows = grad_edge[pl.ds(kind * cap, cap), :].astype(f32)
        edge_done[kind] = (grad_rows + jnp.where(live, through, 0.0)).astype(bf16)

    put(0, first_back, 0)
    put(1, first_back, 1)
    put(2 + odd[0], far_edge, odd[0])
    put(3 - odd[0], near_edge, 1 - odd[0])
    ends = jnp.concatenate([w_in[d : 2 * d, :]] * 2 + [w_in[:d, :]] * 2, axis=1)
    sums = jnp.concatenate([both_halves(unfolded_sums(s[...]), 0) for s in (recv_sum, send0)], axis=0)
    hit_done[...] = (
        grad_hit[...].astype(f32) + dot_nt(node_back[...], wn_in[:d, :]) + dot(ends, sums).T
    )


def closing_kernel(scale, me, mine, theirs, *outs):
    half = mine.shape[0]

    def put(block, start):
        row = 0
        for out in outs:
            low, high = max(row, start), min(row + out.shape[0], start + half)
            if low < high:
                out[low - row : high - row, :] = block[low - start : high - start, :].astype(f32) * scale
            row += out.shape[0]

    @pl.when(me[0] == 0)
    def _():
        put(mine, 0)
        put(theirs, half)

    @pl.when(me[0] != 0)
    def _():
        put(theirs, 0)
        put(mine, half)


def on_device(kernel, outs, operands, flops, scratch=(), scalars=(0,), hbm=False, free=()):
    vmem_spec = pl.BlockSpec(memory_space=pltpu.VMEM)
    smem_spec = pl.BlockSpec(memory_space=pltpu.SMEM)
    in_specs = [smem_spec if i in scalars else vmem_spec for i in range(len(operands))]
    if hbm:
        in_specs = [pl.BlockSpec(memory_space=pltpu.HBM)] * len(operands)
        operands = [pltpu.with_memory_space_constraint(x, pltpu.HBM) for x in operands]
    for i in free:
        in_specs[i] = pl.BlockSpec(memory_space=pl.ANY)
    return pl.pallas_call(
        kernel,
        out_shape=outs,
        in_specs=in_specs,
        out_specs=[vmem_spec] * len(outs),
        scratch_shapes=list(scratch),
        compiler_params=pltpu.CompilerParams(vmem_limit_bytes=VMEM_BYTES),
        cost_estimate=pl.CostEstimate(flops=flops, bytes_accessed=0, transcendentals=0),
    )(*operands)


def summed_over_chips(mine, total, sectors, arrived, finish):
    axes = ("layer", "phi")

    def swap(value, mask):
        return lax.ppermute(value, axes, [(i, i ^ mask) for i in range(total)])

    bits = [1 << b for b in range(total.bit_length() - 1) if 1 << b != sectors]
    near = [1] + [b for b in bits if b > sectors]
    far = [b for b in bits if b not in near]
    ordered = far + near if len(far) % 2 == 0 else near + far
    for at in range(0, len(ordered), 2):
        pair = ordered[at : at + 2]
        masks = pair + [pair[0] ^ pair[1]] if len(pair) == 2 else pair
        sent = mine.astype(bf16)
        mine = sum((swap(sent, m).astype(f32) for m in masks), sent.astype(f32))
        if at == 0:
            beside = finish(arrived)
    mine, beside = lax.optimization_barrier((mine.astype(bf16), beside))
    return mine, swap(mine, sectors), beside


def body(
    hit_features, edge_features, sender_slot, receiver_slot, edge_count, grad_hits, grad_edges,
    w_edge_in, w_edge_out, w_node_in, w_node_out,
):
    hit = hit_features[0, 0]
    nodes, d = hit.shape
    kinds, cap = sender_slot.shape[2:]
    edges, grad_edge = edge_features.reshape(kinds * cap, d), grad_edges.reshape(kinds * cap, d)
    send, recv, counts = sender_slot[0, 0], receiver_slot[0, 0], edge_count[0, 0]
    grad_hit = grad_hits[0, 0]
    layers, sectors = lax.axis_size("layer"), lax.axis_size("phi")
    devices = layers * sectors
    me = (lax.axis_index("layer") % 2).astype(jnp.int32).reshape(1)
    odd = (lax.axis_index("phi") % 2).astype(jnp.int32).reshape(1)
    src2 = shifted(hit, "phi", 1, True)
    src3 = shifted(hit, "phi", -1, True)
    src1 = shifted(lax.optimization_barrier(hit), "layer", 1, False)

    def shape(*dims, dtype=f32):
        return jax.ShapeDtypeStruct(dims, dtype)

    def rows(count):
        return shape(count * cap + SPAN, d)

    def tiles(count):
        return shape(count * cap // SPAN + 1, d, SPAN, dtype=bf16)

    turned = shape(FOLD * d, nodes // FOLD)
    node_half = shape(nodes, d, dtype=bf16)
    (part,) = on_device(
        local_kernel,
        [rows(kinds)],
        (counts, send, recv, hit, edges, w_edge_in),
        4 * 10**9,
        scratch=[
            pltpu.SMEM(counts.shape, jnp.int32),
            pltpu.VMEM(send.shape, jnp.int32),
            pltpu.VMEM(recv.shape, jnp.int32),
            pltpu.VMEM((nodes, d), bf16),
            pltpu.VMEM(edges.shape, bf16),
            pltpu.VMEM(w_edge_in.shape, bf16),
            pltpu.VMEM((1, nodes // FOLD, FOLD * d), bf16),
            pltpu.SemaphoreType.DMA((6,)),
        ],
        hbm=True,
    )
    u0, rs0, hidden0, total = on_device(
        early_kernel,
        [rows(2), rows(2), tiles(2), turned],
        (counts, send, recv, src1, w_edge_in, part),
        2 * 10**9,
        scratch=[
            pltpu.VMEM((1, nodes // FOLD, FOLD * d), bf16),
            pltpu.VMEM((d, FORWARD * SPAN), f32),
        ],
    )
    partial = shape(7 * d, d)
    far_back, far_edge, recv_sum, node_back, inc_grad, partial, u2, rs2, hidden2 = on_device(
        node_kernel,
        [
            node_half, shape(2 * cap + SPAN, d, dtype=bf16),
            turned, node_half, shape(nodes // FOLD, FOLD * d, dtype=bf16), partial,
            rows(2), rows(2), tiles(2),
        ],
        (counts, send, recv, hit, src2, src3, edges, grad_hit, grad_edge,
         w_edge_in, w_edge_out, w_node_in, w_node_out, part, total, odd),
        8 * 10**9,
        scratch=[
            pltpu.VMEM((2, nodes // FOLD, FOLD * d), bf16),
            pltpu.VMEM((1, *turned.shape), f32),
            pltpu.VMEM(turned.shape, f32),
            pltpu.VMEM((d, FORWARD * SPAN), f32),
            pltpu.VMEM((d, BACKWARD * SPAN), f32),
        ],
        scalars=(0, 15),
    )
    route = [(i, (i + (2 if i % 2 else -2)) % sectors) for i in range(sectors)]
    relayed = lax.ppermute(far_back, "phi", route)
    back1, near_back, first_back, near_edge, recv_sum, send0, mine, other = on_device(
        last_kernel,
        [
            node_half, node_half, shape(2 * cap + SPAN, d, dtype=bf16),
            shape(2 * cap + SPAN, d, dtype=bf16), turned, turned,
            shape(7 * d // 2, d), shape(7 * d // 2, d, dtype=bf16),
        ],
        (counts, send, recv, hit, src1, src2, src3, edges, grad_edge, w_edge_in, w_edge_out,
         u0, rs0, hidden0, u2, rs2, hidden2, recv_sum, inc_grad, partial, me, odd),
        8 * 10**9,
        scratch=[
            pltpu.VMEM((3, *turned.shape), f32),
            pltpu.VMEM((7 * d, d), f32),
            pltpu.VMEM((d, BACKWARD * SPAN), f32),
        ],
        scalars=(0, 20, 21),
    )
    other, relayed = lax.optimization_barrier((other, relayed))
    near_back = (near_back.astype(f32) + relayed.astype(f32)).astype(bf16)
    near_back, back1 = lax.optimization_barrier((near_back, back1))
    from_beside = lax.ppermute(near_back, "phi", [(i, i ^ 1) for i in range(sectors)])
    from_upper = shifted(back1, "layer", -1, False)
    mine = mine + lax.ppermute(other, "layer", [(i, i ^ 1) for i in range(layers)]).astype(f32)
    edge_done, hit_done = on_device(
        edge_kernel,
        [shape(kinds, cap, d, dtype=bf16), shape(nodes, d)],
        (counts, grad_hit, grad_edge, w_edge_in, w_node_in,
         first_back, far_edge, near_edge, recv_sum, send0, node_back, odd),
        10**6,
        scalars=(0, 11),
    )

    def hits(from_beside):
        return hit_done + from_upper.astype(f32) + from_beside.astype(f32)

    mine, theirs, hit_total = summed_over_chips(mine, devices, sectors, from_beside, hits)
    summed = on_device(
        functools.partial(closing_kernel, 1.0 / devices),
        [shape(3 * d, d), shape(d, d), shape(2 * d, d), shape(d, d)],
        (me, mine, theirs),
        10**6,
    )
    return (hit_total[None, None], edge_done[None, None], *summed)


def solution(mesh):
    placed = (
        P("layer", "phi", None, None),
        P("layer", "phi", None, None, None),
        P("layer", "phi", None, None),
        P("layer", "phi", None, None),
        P("layer", "phi", None),
        P("layer", "phi", None, None),
        P("layer", "phi", None, None, None),
        P(),
        P(),
        P(),
        P(),
    )
    return jax.shard_map(
        body,
        mesh=mesh,
        in_specs=placed,
        out_specs=(
            P("layer", "phi", None, None),
            P("layer", "phi", None, None, None),
            P(),
            P(),
            P(),
            P(),
        ),
        check_vma=False,
    )
```

```python
import functools

import jax
import jax.numpy as jnp
from jax import lax
from jax.experimental import pallas as pl
from jax.experimental.pallas import tpu as pltpu
from jax.sharding import PartitionSpec as P

norm_eps = 1e-05
bf16, f32 = jnp.bfloat16, jnp.float32
SPAN = 256
FOLD = 4
GROUP = 4
VMEM_BYTES = 16 * 1024 * 1024


def shifted(value, axis, steps, ring):
    count = lax.axis_size(axis)
    if ring:
        route = [(i, (i + steps) % count) for i in range(count)]
    else:
        route = [(i, i + steps) for i in range(count) if 0 <= i + steps < count]
    return lax.ppermute(value, axis, route)


def dot(a, b):
    return jnp.dot(a, b, preferred_element_type=f32)


def dot_nt(a, b):
    return lax.dot_general(a, b, (((1,), (1,)), ((), ())), preferred_element_type=f32)


def dot_tn(a, b):
    return lax.dot_general(a, b, (((0,), (0,)), ((), ())), preferred_element_type=f32)


def halves(x):
    upper = x.astype(bf16)
    return upper, (x - upper.astype(f32)).astype(bf16)


def folded(table):
    width = table.shape[0] // FOLD
    return jnp.concatenate([table[f * width : (f + 1) * width] for f in range(FOLD)], axis=1)


def unfolded_sums(sums):
    d = sums.shape[0] // FOLD
    return jnp.concatenate([sums[f * d : (f + 1) * d] for f in range(FOLD)], axis=1)


class Slots:
    def __init__(self, idx_row, nodes):
        edges = idx_row.shape[1]
        chunks = nodes // FOLD // 128
        block = idx_row >> 7
        self.part = block // chunks
        low = jnp.broadcast_to((idx_row & 127).astype(f32).astype(bf16), (128, edges)).T
        chunk = (block - self.part * chunks).astype(f32).astype(bf16)
        chunk = jnp.broadcast_to(chunk, (128, edges)).T
        self.part_rows = jnp.broadcast_to(self.part.astype(f32), (128, edges)).T
        lane = lax.broadcasted_iota(jnp.int32, (edges, 128), 1).astype(f32).astype(bf16)
        one = jnp.where(low == lane, bf16(1), bf16(0))
        hots = [jnp.where(chunk == bf16(c), one, bf16(0)) for c in range(chunks)]
        self.hot = jnp.concatenate(hots, axis=1)

    def rows(self, table):
        wide = dot(self.hot, table)
        d = wide.shape[1] // FOLD
        out = wide[:, :d]
        for f in range(1, FOLD):
            out = jnp.where(self.part_rows == f, wide[:, f * d : (f + 1) * d], out)
        return out

    def sums(self, turned):
        parts = [jnp.where(self.part == f, turned, 0.0).astype(bf16) for f in range(FOLD)]
        return dot(jnp.concatenate(parts, axis=0), self.hot)


def normed(pre):
    centred = pre - jnp.mean(pre, axis=-1, keepdims=True)
    rstd = lax.rsqrt(jnp.mean(centred * centred, axis=-1, keepdims=True) + norm_eps)
    return centred * rstd, rstd


def gate(u):
    return 1.0 / (1.0 + jnp.exp(-u))


def normed_back(u, rstd, sig, upstream):
    du = upstream * (sig * (1.0 + u * (1.0 - sig)))
    mean_du = jnp.mean(du, axis=-1, keepdims=True)
    mean_duu = jnp.mean(du * u, axis=-1, keepdims=True)
    return rstd * (du - mean_du - u * mean_duu)


class Tiles:
    def __init__(self, counts, kinds, cap, first, held):
        self.kinds, self.cap, self.first, self.held = kinds, cap, first, held
        self.counts = [counts[k] for k in kinds]
        self.ends = []
        end = jnp.int32(0)
        for count in self.counts:
            end = end + (count + SPAN - 1) // SPAN
            self.ends.append(end)

    def place(self, t):
        kind, at, start, count = self.kinds[0], jnp.int32(0), jnp.int32(0), self.counts[0]
        for i in range(1, len(self.kinds)):
            past = t >= self.ends[i - 1]
            kind = jnp.where(past, self.kinds[i], kind)
            at = jnp.where(past, i, at)
            start = jnp.where(past, self.ends[i - 1], start)
            count = jnp.where(past, self.counts[i], count)
        real = t < self.ends[-1]
        offset = jnp.where(real, (t - start) * SPAN, 0)
        rest = jnp.where(real, count - offset, 0)
        row = kind * self.cap + offset
        store = jnp.where(real, row - self.first * self.cap, self.held * self.cap)
        return Place(kind, at, offset, rest, row, row - self.first * self.cap, store)

    def pipelined(self, front, back, held):
        even = self.ends[-1] % GROUP == 0
        choices = ((GROUP, even), (2, ~even)) if held.shape[1] == GROUP * SPAN else ((2, True),)
        for group, wanted in choices:
            steps = jnp.where(wanted, (self.ends[-1] + group - 1) // group, 0)
            now = held.at[:, : group * SPAN]

            def places(i, group=group):
                return [self.place(group * i + j) for j in range(group)]

            def looped(i, carry, now=now, places=places):
                back(places(i - 1), now[...])
                now[...] = front(places(i))
                return carry

            @pl.when(steps > 0)
            def _(steps=steps, now=now, places=places, looped=looped):
                now[...] = front(places(0))
                lax.fori_loop(1, steps, looped, 0)
                back(places(steps - 1), now[...])

    def run(self, step, group=2):
        def looped(i, carry):
            step([self.place(group * i + j) for j in range(group)])
            return carry

        lax.fori_loop(0, (self.ends[-1] + group - 1) // group, looped, 0)


class Place:
    def __init__(self, kind, at, offset, rest, row, own, store):
        self.kind, self.at, self.rest = kind, at, rest
        self.offset = pl.multiple_of(offset, SPAN)
        self.rows = pl.ds(pl.multiple_of(row, SPAN), SPAN)
        self.own = pl.ds(pl.multiple_of(own, SPAN), SPAN)
        self.stored = pl.ds(pl.multiple_of(store, SPAN), SPAN)
        self.tile = store // SPAN

    def slots(self, ref):
        return ref[pl.ds(self.kind, 1), pl.ds(self.offset, SPAN)]


def rows_of(ref, places):
    return jnp.concatenate([ref[p.rows, :] for p in places], axis=0)


def own_rows_of(ref, places):
    return jnp.concatenate([ref[p.own, :] for p in places], axis=0)


def slots_of(ref, places):
    return jnp.concatenate([p.slots(ref) for p in places], axis=1)


def live_of(places, d):
    place = lax.broadcasted_iota(jnp.int32, (SPAN, d), 0)
    return jnp.concatenate([place < p.rest for p in places], axis=0)


def store_rows(ref, places, value):
    for i, p in enumerate(places):
        ref[p.stored, :] = value[i * SPAN : (i + 1) * SPAN]


def receiver_forward(tiles, recv, table, edges, w_in, part):
    nodes, d = table.shape[0] * FOLD, w_in.shape[1]

    def step(places):
        picked = Slots(slots_of(recv, places), nodes).rows(table[...]).astype(bf16)
        pre = dot(picked, w_in[d : 2 * d, :]) + dot(rows_of(edges, places), w_in[2 * d :, :])
        store_rows(part, places, pre)

    tiles.run(step, 4)


def sender_part(places, send, source, w_in):
    nodes, d = source.shape[1] * FOLD, w_in.shape[1]
    picked = [Slots(p.slots(send), nodes).rows(source[p.at]) for p in places]
    return dot(jnp.concatenate(picked, axis=0).astype(bf16), w_in[:d, :])


def forward(tiles, send, recv, source, w_in, part, held, u_all, rs_all, hidden_all, total):
    d = w_in.shape[1]
    nodes = total.shape[1] * FOLD

    def front(places):
        pre = rows_of(part, places)
        if source is not None:
            pre += sender_part(places, send, source, w_in)
        u, rstd = normed(pre)
        store_rows(u_all, places, u)
        store_rows(rs_all, places, jnp.broadcast_to(rstd, u.shape))
        hidden = jnp.where(live_of(places, d), u * gate(u), 0.0).T
        for i, p in enumerate(places):
            hidden_all[p.tile] = hidden[:, i * SPAN : (i + 1) * SPAN].astype(bf16)
        return hidden

    def back(places, hidden):
        total[...] += Slots(slots_of(recv, places), nodes).sums(hidden)

    tiles.pipelined(front, back, held)


def local_kernel(
    counts_far, send_far, recv_far, hit_far, edges_far, w_in_far,
    part,
    counts, send, recv, hit, edges, w_in, table, arrived,
):
    far = (counts_far, send_far, recv_far, hit_far, edges_far, w_in_far)
    near = (counts, send, recv, hit, edges, w_in)
    copies = [pltpu.make_async_copy(f, n, arrived.at[i]) for i, (f, n) in enumerate(zip(far, near))]
    for copy in copies:
        copy.start()
    for copy in copies:
        copy.wait()
    table[0] = folded(hit[...])
    kinds, cap = send.shape
    tiles = Tiles(counts, tuple(range(kinds)), cap, 0, kinds)
    receiver_forward(tiles, recv, table.at[0], edges, w_in, part)

    def step(places):
        store_rows(part, places, rows_of(part, places) + sender_part(places, send, table, w_in))

    Tiles(counts, (0,), cap, 0, kinds).run(step, 4)


def early_kernel(
    counts, send, recv, src1, w_in, part,
    u_all, rs_all, hidden_all, total,
    source, held,
):
    total[...] = jnp.zeros_like(total)
    hidden_all[hidden_all.shape[0] - 1] = jnp.zeros(hidden_all.shape[1:], bf16)
    source[0] = folded(src1[...])
    cap = send.shape[1]
    results = (u_all, rs_all, hidden_all, total)
    forward(Tiles(counts, (0,), cap, 0, 2), send, recv, None, w_in, part, held, *results)
    forward(Tiles(counts, (1,), cap, 0, 2), send, recv, source, w_in, part, held, *results)


def both_halves(x, axis):
    return jnp.concatenate(halves(x), axis=axis)


def backward(
    tiles, send, recv, edges, grad_edge, w_out, inc_grad, u_all, rs_all, hidden_all,
    held, edge_back, recv_sum, send_sum, edge_turned, out_sum,
):
    nodes = inc_grad.shape[0] * FOLD
    d = w_out.shape[0]

    def front(places):
        picked = Slots(slots_of(recv, places), nodes).rows(inc_grad[...])
        live = live_of(places, d)
        grad_rows = rows_of(grad_edge, places).astype(f32)
        message_grad = jnp.where(live, grad_rows + picked, 0.0).astype(bf16)
        hidden_grad = dot_nt(message_grad, w_out[...])
        u = own_rows_of(u_all, places)
        pre_grad = normed_back(u, own_rows_of(rs_all, places), gate(u), hidden_grad)
        pre_grad = jnp.where(live, pre_grad, 0.0)
        store_rows(edge_back, places, pre_grad.astype(bf16))
        hidden = jnp.concatenate([hidden_all[p.tile] for p in places], axis=1)
        out_sum[...] += dot(hidden, message_grad)
        return pre_grad.T

    def back(places, pre_grad):
        recv_sum[...] += Slots(slots_of(recv, places), nodes).sums(pre_grad)
        edge_turned[...] += dot(pre_grad.astype(bf16), rows_of(edges, places))
        for i, p in enumerate(places):
            part_grad = pre_grad[:, i * SPAN : (i + 1) * SPAN]
            send_sum[p.at] += Slots(p.slots(send), nodes).sums(part_grad)

    tiles.pipelined(front, back, held)


def senders_back(send_sum, w_in):
    d = w_in.shape[1]
    w_send = jnp.concatenate([w_in[:d, :], w_in[:d, :]], axis=1)
    return dot(w_send, both_halves(unfolded_sums(send_sum), 0)).T.astype(bf16)


def turned_product(sums, table):
    both = dot(both_halves(unfolded_sums(sums), 0), table)
    d = table.shape[1]
    return both[:d] + both[d:]


def node_kernel(
    counts, send, recv, hit, src2, src3, edges, grad_hit, grad_edge,
    w_in, w_out, wn_in, wn_out, part, total_in, odd,
    far_back, edge_back, recv_sum, node_back, inc_grad, partial, u_all, rs_all, hidden_all,
    source, send_sum, total, held, held_back,
):
    nodes, d = hit.shape
    cap = send.shape[1]
    near = cap // SPAN
    hidden_all[2 * near] = jnp.zeros(hidden_all.shape[1:], bf16)
    total[...] = total_in[...]
    source[0] = folded(src2[...])
    source[1] = folded(src3[...])
    results = (u_all, rs_all, hidden_all, total)
    forward(Tiles(counts, (2, 3), cap, 2, 2), send, recv, source, w_in, part, held, *results)
    upper, lower = halves(unfolded_sums(total[...]).T)
    incoming = (dot(upper, w_out[...]) + dot(lower, w_out[...])).astype(bf16)
    u, rstd = normed(dot(hit[...], wn_in[:d, :]) + dot(incoming, wn_in[d:, :]))
    sig = gate(u)
    hidden = (u * sig).astype(bf16)
    hidden_grad = dot_nt(grad_hit[...], wn_out[...])
    pre_grad = normed_back(u, rstd, sig, hidden_grad).astype(bf16)
    node_back[...] = pre_grad
    inc_grad[...] = folded(dot_nt(pre_grad, wn_in[d:, :]).astype(bf16))
    partial[6 * d : 7 * d, :] = dot_tn(hidden, grad_hit[...])
    partial[4 * d : 5 * d, :] = dot_tn(hit[...], pre_grad)
    partial[5 * d : 6 * d, :] = dot_tn(incoming, pre_grad)
    partial[2 * d : 4 * d, :] = jnp.zeros((2 * d, d), f32)
    recv_sum[...] = jnp.zeros_like(recv_sum)
    send_sum[...] = jnp.zeros_like(send_sum)
    backward(
        Tiles(counts, (2 + odd[0],), cap, 2, 2), send, recv, edges, grad_edge, w_out, inc_grad,
        u_all, rs_all, hidden_all, held_back, edge_back, recv_sum, send_sum,
        partial.at[2 * d : 3 * d], partial.at[3 * d : 4 * d],
    )
    far = jnp.where(odd[0] == 1, src3[...].astype(f32), src2[...].astype(f32)).astype(bf16)
    partial[:d, :] = turned_product(send_sum[0], far)
    far_back[...] = senders_back(send_sum[0], w_in)


def last_kernel(
    counts, send, recv, hit, src1, src2, src3, edges, grad_edge, w_in, w_out,
    u0, rs0, hidden0, u2, rs2, hidden2, recv_in, inc_grad, partial, me, odd,
    back1, near_back, edge_back, near_edge, recv_sum, send0, mine, other,
    send_sum, weights, held,
):
    cap, d = send.shape[1], hit.shape[1]
    weights[...] = partial[...]
    recv_sum[...] = recv_in[...]
    send_sum[...] = jnp.zeros_like(send_sum)
    backward(
        Tiles(counts, (0, 1), cap, 0, 2), send, recv, edges, grad_edge, w_out, inc_grad,
        u0, rs0, hidden0, held, edge_back, recv_sum, send_sum,
        weights.at[2 * d : 3 * d], weights.at[3 * d : 4 * d],
    )
    backward(
        Tiles(counts, (3 - odd[0],), cap, 2, 2), send, recv, edges, grad_edge, w_out, inc_grad,
        u2, rs2, hidden2, held, near_edge, recv_sum, send_sum.at[2:],
        weights.at[2 * d : 3 * d], weights.at[3 * d : 4 * d],
    )
    near = jnp.where(odd[0] == 1, src2[...].astype(f32), src3[...].astype(f32)).astype(bf16)
    near_back[...] = senders_back(send_sum[2], w_in)
    turned = turned_product(send_sum[0], hit[...]) + turned_product(send_sum[1], src1[...])
    turned += turned_product(send_sum[2], near)
    weights[:d, :] = (weights[:d, :] + turned).T
    weights[d : 2 * d, :] = turned_product(recv_sum[...], hit[...]).T
    weights[2 * d : 3 * d, :] = weights[2 * d : 3 * d, :].T
    back1[...] = senders_back(send_sum[1], w_in)
    send0[...] = send_sum[0]
    half = mine.shape[0]
    mine[...] = weights[pl.ds(pl.multiple_of(me[0] * half, half), half), :]
    other[...] = weights[pl.ds(pl.multiple_of((1 - me[0]) * half, half), half), :].astype(bf16)


def edge_kernel(
    counts, grad_hit, grad_edge, w_in, wn_in, first_back, far_edge, near_edge, recv_sum, send0, node_back, odd,
    edge_done, hit_done,
):
    d = w_in.shape[1]
    cap = edge_done.shape[1]

    def put(kind, back, row):
        through = dot_nt(back[pl.ds(row * cap, cap), :], w_in[2 * d :, :])
        live = lax.broadcasted_iota(jnp.int32, through.shape, 0) < counts[kind]
        grad_rows = grad_edge[pl.ds(kind * cap, cap), :].astype(f32)
        edge_done[kind] = (grad_rows + jnp.where(live, through, 0.0)).astype(bf16)

    put(0, first_back, 0)
    put(1, first_back, 1)
    put(2 + odd[0], far_edge, odd[0])
    put(3 - odd[0], near_edge, 1 - odd[0])
    ends = jnp.concatenate([w_in[d : 2 * d, :]] * 2 + [w_in[:d, :]] * 2, axis=1)
    sums = jnp.concatenate([both_halves(unfolded_sums(s[...]), 0) for s in (recv_sum, send0)], axis=0)
    hit_done[...] = (
        grad_hit[...].astype(f32) + dot_nt(node_back[...], wn_in[:d, :]) + dot(ends, sums).T
    )


def closing_kernel(scale, me, mine, theirs, *outs):
    half = mine.shape[0]

    def put(block, start):
        row = 0
        for out in outs:
            low, high = max(row, start), min(row + out.shape[0], start + half)
            if low < high:
                out[low - row : high - row, :] = block[low - start : high - start, :].astype(f32) * scale
            row += out.shape[0]

    @pl.when(me[0] == 0)
    def _():
        put(mine, 0)
        put(theirs, half)

    @pl.when(me[0] != 0)
    def _():
        put(theirs, 0)
        put(mine, half)


def on_device(kernel, outs, operands, flops, scratch=(), scalars=(0,), hbm=False, free=()):
    vmem_spec = pl.BlockSpec(memory_space=pltpu.VMEM)
    smem_spec = pl.BlockSpec(memory_space=pltpu.SMEM)
    in_specs = [smem_spec if i in scalars else vmem_spec for i in range(len(operands))]
    if hbm:
        in_specs = [pl.BlockSpec(memory_space=pltpu.HBM)] * len(operands)
        operands = [pltpu.with_memory_space_constraint(x, pltpu.HBM) for x in operands]
    for i in free:
        in_specs[i] = pl.BlockSpec(memory_space=pl.ANY)
    return pl.pallas_call(
        kernel,
        out_shape=outs,
        in_specs=in_specs,
        out_specs=[vmem_spec] * len(outs),
        scratch_shapes=list(scratch),
        compiler_params=pltpu.CompilerParams(vmem_limit_bytes=VMEM_BYTES),
        cost_estimate=pl.CostEstimate(flops=flops, bytes_accessed=0, transcendentals=0),
    )(*operands)


def summed_over_chips(mine, total, sectors, arrived, finish):
    axes = ("layer", "phi")

    def swap(value, mask):
        return lax.ppermute(value, axes, [(i, i ^ mask) for i in range(total)])

    bits = [1 << b for b in range(total.bit_length() - 1) if 1 << b != sectors]
    near = [1] + [b for b in bits if b > sectors]
    far = [b for b in bits if b not in near]
    ordered = far + near if len(far) % 2 == 0 else near + far
    for at in range(0, len(ordered), 2):
        pair = ordered[at : at + 2]
        masks = pair + [pair[0] ^ pair[1]] if len(pair) == 2 else pair
        sent = mine.astype(bf16)
        mine = sum((swap(sent, m).astype(f32) for m in masks), sent.astype(f32))
        if at == 0:
            beside = finish(arrived)
    mine, beside = lax.optimization_barrier((mine.astype(bf16), beside))
    return mine, swap(mine, sectors), beside


def body(
    hit_features, edge_features, sender_slot, receiver_slot, edge_count, grad_hits, grad_edges,
    w_edge_in, w_edge_out, w_node_in, w_node_out,
):
    hit = hit_features[0, 0]
    nodes, d = hit.shape
    kinds, cap = sender_slot.shape[2:]
    edges, grad_edge = edge_features.reshape(kinds * cap, d), grad_edges.reshape(kinds * cap, d)
    send, recv, counts = sender_slot[0, 0], receiver_slot[0, 0], edge_count[0, 0]
    grad_hit = grad_hits[0, 0]
    layers, sectors = lax.axis_size("layer"), lax.axis_size("phi")
    devices = layers * sectors
    me = (lax.axis_index("layer") % 2).astype(jnp.int32).reshape(1)
    odd = (lax.axis_index("phi") % 2).astype(jnp.int32).reshape(1)
    src2 = shifted(hit, "phi", 1, True)
    src3 = shifted(hit, "phi", -1, True)
    src1 = shifted(lax.optimization_barrier(hit), "layer", 1, False)

    def shape(*dims, dtype=f32):
        return jax.ShapeDtypeStruct(dims, dtype)

    def rows(count):
        return shape(count * cap + SPAN, d)

    def tiles(count):
        return shape(count * cap // SPAN + 1, d, SPAN, dtype=bf16)

    turned = shape(FOLD * d, nodes // FOLD)
    node_half = shape(nodes, d, dtype=bf16)
    (part,) = on_device(
        local_kernel,
        [rows(kinds)],
        (counts, send, recv, hit, edges, w_edge_in),
        4 * 10**9,
        scratch=[
            pltpu.SMEM(counts.shape, jnp.int32),
            pltpu.VMEM(send.shape, jnp.int32),
            pltpu.VMEM(recv.shape, jnp.int32),
            pltpu.VMEM((nodes, d), bf16),
            pltpu.VMEM(edges.shape, bf16),
            pltpu.VMEM(w_edge_in.shape, bf16),
            pltpu.VMEM((1, nodes // FOLD, FOLD * d), bf16),
            pltpu.SemaphoreType.DMA((6,)),
        ],
        hbm=True,
    )
    u0, rs0, hidden0, total = on_device(
        early_kernel,
        [rows(2), rows(2), tiles(2), turned],
        (counts, send, recv, src1, w_edge_in, part),
        2 * 10**9,
        scratch=[
            pltpu.VMEM((1, nodes // FOLD, FOLD * d), bf16),
            pltpu.VMEM((d, 2 * SPAN), f32),
        ],
    )
    partial = shape(7 * d, d)
    far_back, far_edge, recv_sum, node_back, inc_grad, partial, u2, rs2, hidden2 = on_device(
        node_kernel,
        [
            node_half, shape(2 * cap + SPAN, d, dtype=bf16),
            turned, node_half, shape(nodes // FOLD, FOLD * d, dtype=bf16), partial,
            rows(2), rows(2), tiles(2),
        ],
        (counts, send, recv, hit, src2, src3, edges, grad_hit, grad_edge,
         w_edge_in, w_edge_out, w_node_in, w_node_out, part, total, odd),
        8 * 10**9,
        scratch=[
            pltpu.VMEM((2, nodes // FOLD, FOLD * d), bf16),
            pltpu.VMEM((1, *turned.shape), f32),
            pltpu.VMEM(turned.shape, f32),
            pltpu.VMEM((d, GROUP * SPAN), f32),
            pltpu.VMEM((d, GROUP * SPAN), f32),
        ],
        scalars=(0, 15),
    )
    route = [(i, (i + (2 if i % 2 else -2)) % sectors) for i in range(sectors)]
    relayed = lax.ppermute(far_back, "phi", route)
    back1, near_back, first_back, near_edge, recv_sum, send0, mine, other = on_device(
        last_kernel,
        [
            node_half, node_half, shape(2 * cap + SPAN, d, dtype=bf16),
            shape(2 * cap + SPAN, d, dtype=bf16), turned, turned,
            shape(7 * d // 2, d), shape(7 * d // 2, d, dtype=bf16),
        ],
        (counts, send, recv, hit, src1, src2, src3, edges, grad_edge, w_edge_in, w_edge_out,
         u0, rs0, hidden0, u2, rs2, hidden2, recv_sum, inc_grad, partial, me, odd),
        8 * 10**9,
        scratch=[
            pltpu.VMEM((3, *turned.shape), f32),
            pltpu.VMEM((7 * d, d), f32),
            pltpu.VMEM((d, 2 * SPAN), f32),
        ],
        scalars=(0, 20, 21),
    )
    other, relayed = lax.optimization_barrier((other, relayed))
    near_back = (near_back.astype(f32) + relayed.astype(f32)).astype(bf16)
    near_back, back1 = lax.optimization_barrier((near_back, back1))
    from_beside = lax.ppermute(near_back, "phi", [(i, i ^ 1) for i in range(sectors)])
    from_upper = shifted(back1, "layer", -1, False)
    mine = mine + lax.ppermute(other, "layer", [(i, i ^ 1) for i in range(layers)]).astype(f32)
    edge_done, hit_done = on_device(
        edge_kernel,
        [shape(kinds, cap, d, dtype=bf16), shape(nodes, d)],
        (counts, grad_hit, grad_edge, w_edge_in, w_node_in,
         first_back, far_edge, near_edge, recv_sum, send0, node_back, odd),
        10**6,
        scalars=(0, 11),
    )

    def hits(from_beside):
        return hit_done + from_upper.astype(f32) + from_beside.astype(f32)

    mine, theirs, hit_total = summed_over_chips(mine, devices, sectors, from_beside, hits)
    summed = on_device(
        functools.partial(closing_kernel, 1.0 / devices),
        [shape(3 * d, d), shape(d, d), shape(2 * d, d), shape(d, d)],
        (me, mine, theirs),
        10**6,
    )
    return (hit_total[None, None], edge_done[None, None], *summed)


def solution(mesh):
    placed = (
        P("layer", "phi", None, None),
        P("layer", "phi", None, None, None),
        P("layer", "phi", None, None),
        P("layer", "phi", None, None),
        P("layer", "phi", None),
        P("layer", "phi", None, None),
        P("layer", "phi", None, None, None),
        P(),
        P(),
        P(),
        P(),
    )
    return jax.shard_map(
        body,
        mesh=mesh,
        in_specs=placed,
        out_specs=(
            P("layer", "phi", None, None),
            P("layer", "phi", None, None, None),
            P(),
            P(),
            P(),
            P(),
        ),
        check_vma=False,
    )
```
